32 devices in a mesh: row: 4 (over x, core), col: 8 (over z, y).
Axes of the slice: x: 2, y: 2, z: 4, core: 2. Of those that a mesh axis runs over, the one named last changes fastest.
Arguments:
- features: bfloat16 [8192, 512], P('col', 'row'), may hold values from -6 to 6
- weight: bfloat16 [512, 512], replicated, may hold values from -0.25 to 0.25
- bias: float32 [512], replicated, may hold values from -3 to 3
- edge_src: int32 [64, 4096], P('row', 'col'), may hold values from 0 to 1023
- edge_dst: int32 [64, 4096], P('row', 'col'), may hold values from 0 to 127
- tile_count: int32 [64, 8], P('row', 'col'), may hold values from 0 to 512, as said below
Outputs:
- layer_out: bfloat16 [8192, 512], P(('row', 'col'))
The draws below stay inside these ranges and needn't reach their ends.
Inputs may be any that keep to these rules, and one draw needn't show every extreme that they name: `tile_count`: entries of a tile past its count are padding and carry no edge. Some tile holds exactly 512 live edges from one sending block in every draw.
All inputs are finite; a program needn't handle non-finite values.
Results may differ from the reference program's by a relative error of at most 0.0034.
Values may be sent and summed in bfloat16 or wider, within the bound.
No kernel may reach another device: no remote copies, remote signals or barrier semaphores. Data moves between devices by JAX's collectives and lax.ppermute only.
A program may use at most 128 MiB of HBM per device.

```python
import math
import jax
import jax.numpy as jnp
import numpy as np
from jax import lax

F = 512
TILE = 128
EDGE_CAP = 512
NODES = 8192
TILES = 64
BLOCK_ROWS = 2048
SRC_ROWS = 1024
N_COL = 8


def draw_tile_count(key, part):
    column_count = NODES // SRC_ROWS
    row_count = NODES // BLOCK_ROWS
    key_one, key_two, key_three = jax.random.split(key, 3)
    tile_index = jnp.arange(TILES, dtype=jnp.int32)[:, None]
    column = jnp.arange(column_count, dtype=jnp.int32)[None, :]
    row_block = tile_index // (TILES // row_count)
    limit_cap = EDGE_CAP * (row_count - 1 + 2 * row_block) * (column_count - 1 + 2 * column) // (9 * (row_count - 1) * (column_count - 1))
    limit_cap = jnp.maximum(limit_cap, 1)
    first_draw = jax.random.randint(key_one, (TILES, column_count), 0, EDGE_CAP + 1)
    second_draw = jax.random.randint(key_two, (TILES, column_count), 0, EDGE_CAP + 1)
    reduction = limit_cap * (first_draw * second_draw // (EDGE_CAP + 1)) // (EDGE_CAP + 1)
    counts = limit_cap - reduction
    chosen = jax.random.randint(key_three, (), TILES - TILES // row_count, TILES)
    full_slot = (tile_index == chosen) & (column == column_count - 1)
    return jnp.where(full_slot, EDGE_CAP, counts).astype(jnp.int32)


def set_ends(result, stream_key, low, top_value):
    longest = result.shape.index(max(result.shape))
    spots = []
    for shift in (0, 1):
        where = [jax.random.randint(jax.random.fold_in(stream_key, axis), (), 0, length) for axis, length in enumerate(result.shape)]
        where[longest] = (where[longest] + shift) % result.shape[longest]
        spots.append(tuple(where))
    return result.at[spots[0]].set(low).at[spots[1]].set(top_value)


def block_levels(key, shape, pieces, low, largest):
    loudness = 1.0
    for axis_at, blocks in pieces:
        steps = jax.random.uniform(jax.random.fold_in(jax.random.fold_in(key, 6), axis_at), (blocks,), jnp.float32, low / len(pieces), largest / len(pieces))
        loudness = loudness * jnp.repeat(jnp.exp(steps), shape[axis_at] // blocks).reshape((-1,) + (1,) * (len(shape) - 1 - axis_at))
    return loudness


def cumulative_ranks(number_of, skew):
    loads = [(1 << 20) // math.isqrt(rank ** skew) + 1 for rank in range(1, number_of + 1)]
    scale = 1 + sum(loads) // (1 << 30)
    return np.cumsum(np.array([max(1, weight // scale) for weight in loads]))


def ranked_ids(stream_key, dims, number_of, skew):
    listing = cumulative_ranks(number_of, skew)
    pick = jax.random.randint(jax.random.fold_in(stream_key, 1), dims, 0, int(listing[number_of - 1]))
    grade = jnp.searchsorted(jnp.asarray(listing, jnp.int32), pick, side="right")
    return jax.random.permutation(jax.random.fold_in(stream_key, 2), number_of)[grade].astype(jnp.int32)


def centred(key, extent, spread, limit, cuts=(), held_as=jnp.bfloat16):
    level = block_levels(key, extent, cuts, -0.22, 0.18) if cuts else 1.0
    values = jax.random.normal(key, extent, jnp.float32) * spread * level
    return jnp.minimum(jnp.maximum(values, -limit), limit).astype(held_as)


def setup_inputs(seed: int = 0) -> dict:
    keys = jax.random.split(jax.random.key(seed), 7)
    return {
        "features": centred(keys[0], (NODES, F), 1.0, 6.0, ((0, 8), (1, 4))),
        "weight": centred(keys[1], (F, F), F ** -0.5, 0.25),
        "bias": centred(keys[2], (F,), 0.5, 3.0, (), jnp.float32),
        "edge_src": set_ends(ranked_ids(keys[3], (TILES, N_COL * EDGE_CAP), SRC_ROWS, 2), jax.random.fold_in(keys[3], 3), 0, SRC_ROWS - 1).astype(jnp.int32),
        "edge_dst": set_ends(jax.random.randint(keys[4], (TILES, N_COL * EDGE_CAP), 0, TILE), jax.random.fold_in(keys[4], 1), 0, TILE - 1).astype(jnp.int32),
        "tile_count": draw_tile_count(jax.random.fold_in(keys[6], 71), 0),
    }


def reference(features, weight, bias, edge_src, edge_dst, tile_count):
    node_total, feat_width = features.shape
    tile_total, slot_total = edge_src.shape
    block_count = tile_count.shape[1]
    slot_cap = slot_total // block_count
    slot_index = jnp.arange(slot_total, dtype=jnp.int32)
    block_of = slot_index // slot_cap
    within = slot_index - block_of * slot_cap
    limits = jnp.repeat(tile_count, slot_cap, axis=1)
    live_mask = (within[None, :] < limits).astype(jnp.float32)
    source_all = block_of[None, :] * (node_total // block_count) + edge_src
    tile_base = jnp.arange(tile_total, dtype=jnp.int32)[:, None] * TILE
    target_all = tile_base + edge_dst
    out_degree = jnp.zeros((node_total,), jnp.float32).at[source_all.reshape(-1)].add(live_mask.reshape(-1))
    in_degree = jnp.zeros((node_total,), jnp.float32).at[target_all.reshape(-1)].add(live_mask.reshape(-1))
    scaled = (features.astype(jnp.float32) * lax.rsqrt(1.0 + out_degree)[:, None]).astype(jnp.bfloat16)

    def one_tile(packed):
        source, target, weights = packed
        values = scaled[source].astype(jnp.float32) * weights[:, None]
        return jnp.zeros((TILE, feat_width), jnp.float32).at[target].add(values)
    aggregate = lax.map(one_tile, (source_all, edge_dst, live_mask)).reshape(node_total, feat_width)
    normed = (aggregate * lax.rsqrt(1.0 + in_degree)[:, None]).astype(jnp.bfloat16)
    projected = jnp.dot(normed, weight, preferred_element_type=jnp.float32) + bias
    return jax.nn.relu(projected).astype(jnp.bfloat16)
```

```python
import functools

import jax
import jax.numpy as jnp
from jax import lax
from jax.experimental import pallas as pl
from jax.experimental.pallas import tpu as pltpu
from jax.sharding import PartitionSpec as P

TILE = 128
LANES = 128
LOW = 256
NT = (((1,), (1,)), ((), ()))
BITS8 = jnp.float8_e4m3fn


def flag(condition):
    return jnp.where(condition, 1.0, 0.0).astype(jnp.bfloat16)


def short(whole):
    return whole.astype(jnp.float32).astype(jnp.bfloat16)


def equal(ids, whole):
    return jnp.where(ids == short(whole), jnp.bfloat16(1), jnp.bfloat16(0))


def pack_kernel(src_ref, dst_ref, count_ref, out_ref, lines):
    tiles, cap = src_ref.shape
    rows, cols, depth, _ = out_ref.shape
    subs = cap // LANES
    own = tiles // cols * subs // 2
    high = 2 * (depth - own)
    src = src_ref[...]
    tile_ids = lax.broadcasted_iota(jnp.int32, (tiles, cap), 0)
    count = jnp.zeros((tiles, cap), jnp.int32)
    for t in range(tiles):
        count = jnp.where(tile_ids == t, count_ref[t], count)
    live = lax.broadcasted_iota(jnp.int32, (tiles, cap), 1) < count
    packed = src + jnp.where(live, dst_ref[...], TILE) * 65536
    for j in range(subs):
        lines[pl.ds(j, tiles, stride=subs), :] = packed[:, j * LANES : (j + 1) * LANES]
    edges = lines[...].reshape(cols, 2 * own, LANES)
    for r in range(rows):
        first = r % 2 * own
        out_ref[r, :, :own, :] = edges[:, first : first + own, :]
    src_high = jnp.where(live, src // LANES, high)
    src_low = src % LANES
    high_ids = lax.broadcasted_iota(jnp.int32, (high, cap), 0)
    low_ids = lax.broadcasted_iota(jnp.int32, (LANES, cap), 0)
    total = jnp.zeros((high, LANES), jnp.float32)
    for t in range(tiles):
        total += lax.dot_general(
            flag(high_ids == src_high[t : t + 1]),
            flag(low_ids == src_low[t : t + 1]),
            NT,
            preferred_element_type=jnp.float32,
        )
    degree = total.astype(jnp.int32)
    for r in range(rows):
        first = r % 2 * (high // 2)
        out_ref[r, :, own:, :] = jnp.broadcast_to(
            degree[first : first + high // 2], (cols, high // 2, LANES)
        )


def ring_col_of(place, cols):
    return 2 * place if place < cols // 2 else 2 * (cols - 1 - place) + 1


def ring_place(col, cols):
    return jnp.where(col % 2 == 0, col // 2, cols - 1 - col // 2)


def ring_col(place, cols):
    return jnp.where(place < cols // 2, 2 * place, 2 * (cols - 1 - place) + 1)


def sum_kernel(cols, shifts, groups, first, last, col_ref, *refs):
    row_ref, *refs = refs
    edge_refs, refs = refs[:2], refs[2:]
    xs, refs = refs[: sum(groups)], refs[sum(groups) :]
    if not first:
        old_ref, *refs = refs
    rows, _, depth, _ = edge_refs[0].shape
    out_refs, refs = refs[: rows if last else 1], refs[rows if last else 1 :]
    counts, scaled, *refs = refs
    total = refs[0] if last else out_refs[0]
    width = xs[0].shape[1]
    _, sums, src_rows = counts.shape
    highs = src_rows // LOW
    own = depth - src_rows // LANES // 2
    tiles = sums // rows // TILE // 2
    subs = own // tiles
    odd = lax.rem(row_ref[0], 2)
    place = ring_place(col_ref[0], cols)
    blocks = [ring_col(lax.rem(place + shift + cols, cols), cols) for shift in shifts]
    diagonal = lax.broadcasted_iota(jnp.int32, (LANES, LANES), 0) == lax.broadcasted_iota(
        jnp.int32, (LANES, LANES), 1
    )
    target_ids = short(lax.broadcasted_iota(jnp.int32, (TILE, LANES), 0))
    low_ids = short(lax.broadcasted_iota(jnp.int32, (LOW, LANES), 0))

    def put_scaled(g):
        halves = [
            sum(edge_ref[r, blocks[g], own:, :] for r in range(rows)).astype(jnp.float32)
            for edge_ref in edge_refs
        ]
        degree = jnp.where(odd == 0, jnp.concatenate(halves), jnp.concatenate(halves[::-1]))
        scale = lax.rsqrt(1.0 + degree)
        top = 0
        for x_ref in xs[sum(groups[:g]) : sum(groups[: g + 1])]:
            for i in range(x_ref.shape[0] // LANES):
                row = scale[top // LANES : top // LANES + 1]
                column = jnp.sum(jnp.where(diagonal, row, 0.0), axis=1, keepdims=True)
                x = x_ref[i * LANES : (i + 1) * LANES, :].astype(jnp.float32)
                scaled[g % 2, top : top + LANES, :width] = (x * column).astype(jnp.bfloat16)
                top += LANES

    def count_block(g, edge_ref, r, t):
        lefts, rights = [], []
        for j in range(subs):
            edges = edge_ref[r, blocks[g], pl.ds(t * subs + j, 1), :]
            src = edges & 65535
            target_one = equal(target_ids, edges >> 16)
            src_high = src // LOW
            left = [target_one * flag(src_high == h) for h in range(highs)]
            lefts.append(jnp.concatenate(left, axis=0).astype(BITS8))
            rights.append(equal(low_ids, src % LOW).astype(BITS8))
        return lax.dot_general(
            jnp.concatenate(lefts, axis=1),
            jnp.concatenate(rights, axis=1),
            NT,
            preferred_element_type=jnp.float32,
        )

    def add_block(g, convert, unroll):
        def fill_tile(part, i, carry):
            r, t = i // tiles, i % tiles
            block = count_block(g, edge_refs[part], r, t)
            half = 1 - odd if part else odd
            top = pl.multiple_of(((2 * r + half) * tiles + t) * TILE, TILE)
            for h in range(highs):
                counts[g % 2, pl.ds(top, TILE), h * LOW : (h + 1) * LOW] = convert(
                    block[h * TILE : (h + 1) * TILE]
                )
            return carry

        put_scaled(g)
        for part in range(2):
            if unroll:
                for i in range(rows * tiles):
                    fill_tile(part, i, 0)
            else:
                lax.fori_loop(0, rows * tiles, functools.partial(fill_tile, part), 0)
        total[...] += jnp.dot(counts[g % 2], scaled[g % 2], preferred_element_type=jnp.float32)

    scaled[...] = jnp.ones_like(scaled)
    total[...] = jnp.zeros_like(total) if first else old_ref[...]
    for g in range(len(groups)):
        add_block(g, lambda block: block.astype(jnp.bfloat16), rows * tiles <= 4)

    @pl.when(jnp.max(total[:, LANES:]) >= 256.0)
    def _():
        for g in range(len(groups)):
            add_block(
                g,
                lambda block: (block - block.astype(jnp.bfloat16).astype(jnp.float32)).astype(jnp.bfloat16),
                False,
            )

    if last:
        for shift, out_ref in enumerate(out_refs):
            size = out_ref.shape[0]
            part = pl.ds(pl.multiple_of(lax.rem(row_ref[0] + shift, rows) * size, size), size)
            norm = lax.rsqrt(1.0 + total[part, LANES : LANES + width])
            out_ref[...] = (total[part, :width] * norm).astype(jnp.bfloat16)


def layer_kernel(row_ref, *refs):
    *x_refs, weight_ref, bias_hbm, out_ref, bias, arrived = refs
    copy = pltpu.make_async_copy(bias_hbm, bias, arrived)
    copy.start()
    rows, width = len(x_refs), x_refs[0].shape[1]
    projected = None
    for shift, x_ref in enumerate(x_refs):
        top = pl.multiple_of(lax.rem(row_ref[0] - shift + rows, rows) * width, width)
        part = jnp.dot(x_ref[...], weight_ref[pl.ds(top, width), :], preferred_element_type=jnp.float32)
        projected = part if projected is None else projected + part
    copy.wait()
    out_ref[...] = jnp.maximum(projected + bias[...], 0.0).astype(jnp.bfloat16)


def body(rows, cols, features, weight, bias, edge_src, edge_dst, tile_count):
    tiles, cap = edge_src.shape
    src_rows, width = features.shape
    hidden = weight.shape[1]
    degree_rows = src_rows // LANES
    own_rows = tiles * cap // LANES // cols
    own_nodes = tiles // cols * TILE
    sums = rows * own_nodes
    order = [ring_col_of(place, cols) for place in range(cols)]
    ahead = [(order[p], order[(p + 1) % cols]) for p in range(cols)]
    back = [(order[(p + 1) % cols], order[p]) for p in range(cols)]
    half = src_rows // 2

    depth = (own_rows + degree_rows) // 2
    packed = pl.pallas_call(
        pack_kernel,
        in_specs=[pl.BlockSpec(), pl.BlockSpec(), pl.BlockSpec(memory_space=pltpu.SMEM)],
        out_shape=jax.ShapeDtypeStruct((rows, cols, depth, LANES), jnp.int32),
        scratch_shapes=[pltpu.VMEM((cols * own_rows, LANES), jnp.int32)],
    )(edge_src, edge_dst, tile_count.reshape(tiles))
    edges = lax.all_to_all(
        packed.reshape(rows * cols, depth, LANES),
        ("row", "col"),
        split_axis=0,
        concat_axis=0,
        tiled=True,
    )
    other = lax.ppermute(edges, "row", [(r, r + 1 - 2 * (r % 2)) for r in range(rows)])
    edges = [half.reshape(rows, cols, depth, LANES) for half in (edges, other)]
    col = lax.axis_index("col").astype(jnp.int32).reshape(1)
    row = lax.axis_index("row").astype(jnp.int32).reshape(1)

    def add_blocks(total, blocks, last, flops):
        first = total is None
        shifts = [shift for shift, _ in blocks]
        groups = [len(pieces) for _, pieces in blocks]
        pieces = [piece for _, listed in blocks for piece in listed]

        whole = lambda array: pl.BlockSpec(array.shape, lambda i, c, r: (0,) * array.ndim)
        operands = pieces + ([] if first else [total])
        out_shape = (
            [jax.ShapeDtypeStruct((own_nodes, width), jnp.bfloat16)] * rows
            if last
            else [jax.ShapeDtypeStruct((sums, 2 * LANES), jnp.float32)]
        )
        scratch = [
            pltpu.VMEM((2, sums, src_rows), jnp.bfloat16),
            pltpu.VMEM((2, src_rows, 2 * LANES), jnp.bfloat16),
        ]
        if last:
            scratch.append(pltpu.VMEM((sums, 2 * LANES), jnp.float32))
        return pl.pallas_call(
            functools.partial(sum_kernel, cols, shifts, groups, first, last),
            grid_spec=pltpu.PrefetchScalarGridSpec(
                num_scalar_prefetch=2,
                grid=(1,),
                in_specs=[whole(operand) for operand in edges + operands],
                out_specs=[whole(array) for array in out_shape],
                scratch_shapes=scratch,
            ),
            out_shape=out_shape,
            compiler_params=pltpu.CompilerParams(vmem_limit_bytes=48 * 1024 * 1024),
            cost_estimate=pl.CostEstimate(flops=flops, bytes_accessed=2**22, transcendentals=0),
        )(col, row, *edges, *operands)

    block_flops = 2 * sums * src_rows * (2 * LANES + cap)
    ups = downs = features
    total, waiting = None, [(0, [features])]
    for hop in range(1, cols // 2):
        ups = lax.ppermute(ups, "col", ahead)
        downs = lax.ppermute(downs, "col", back)
        waiting += [(-hop, [ups]), (hop, [downs])]
        if hop > 1:
            (total,) = add_blocks(total, waiting, False, 2 * len(waiting) * block_flops)
            waiting = []
    ups = lax.ppermute(ups[:half], "col", ahead)
    downs = lax.ppermute(downs[half:], "col", back)
    waiting.append((cols // 2, [ups, downs]))
    normed = list(add_blocks(total, waiting, True, block_flops))
    for shift in range(1, rows):
        pairs = [(r, (r + shift) % rows) for r in range(rows)]
        normed[shift] = lax.ppermute(normed[shift], "row", pairs)
    operands = [*normed, weight]
    return pl.pallas_call(
        layer_kernel,
        grid_spec=pltpu.PrefetchScalarGridSpec(
            num_scalar_prefetch=1,
            grid=(1,),
            in_specs=[pl.BlockSpec(array.shape, lambda i, r: (0, 0)) for array in operands]
            + [pl.BlockSpec(memory_space=pl.ANY)],
            out_specs=pl.BlockSpec((own_nodes, hidden), lambda i, r: (0, 0)),
            scratch_shapes=[pltpu.VMEM((1, hidden), jnp.float32), pltpu.SemaphoreType.DMA],
        ),
        out_shape=jax.ShapeDtypeStruct((own_nodes, hidden), jnp.bfloat16),
        compiler_params=pltpu.CompilerParams(vmem_limit_bytes=8 * 1024 * 1024),
    )(row, *operands, bias.reshape(1, hidden))


def solution(mesh):
    rows, cols = mesh.shape["row"], mesh.shape["col"]
    in_specs = (P("col", "row"), P(), P(), P("row", "col"), P("row", "col"), P("row", "col"))
    out_specs = P(("row", "col"), None)
    return jax.shard_map(
        functools.partial(body, rows, cols),
        mesh=mesh,
        in_specs=in_specs,
        out_specs=out_specs,
        check_vma=False,
    )
```

```python
import functools

import jax
import jax.numpy as jnp
from jax import lax
from jax.experimental import pallas as pl
from jax.experimental.pallas import tpu as pltpu
from jax.sharding import PartitionSpec as P

TILE = 128
LANES = 128
LOW = 256
NT = (((1,), (1,)), ((), ()))
BITS8 = jnp.float8_e4m3fn


def flag(condition):
    return jnp.where(condition, 1.0, 0.0).astype(jnp.bfloat16)


def short(whole):
    return whole.astype(jnp.float32).astype(jnp.bfloat16)


def equal(ids, whole):
    return jnp.where(ids == short(whole), jnp.bfloat16(1), jnp.bfloat16(0))


def pack_kernel(src_ref, dst_ref, count_ref, out_ref, lines):
    tiles, cap = src_ref.shape
    rows, cols, depth, _ = out_ref.shape
    subs = cap // LANES
    own = tiles // cols * subs // 2
    high = 2 * (depth - own)
    src = src_ref[...]
    tile_ids = lax.broadcasted_iota(jnp.int32, (tiles, cap), 0)
    count = jnp.zeros((tiles, cap), jnp.int32)
    for t in range(tiles):
        count = jnp.where(tile_ids == t, count_ref[t], count)
    live = lax.broadcasted_iota(jnp.int32, (tiles, cap), 1) < count
    packed = src + jnp.where(live, dst_ref[...], TILE) * 65536
    for j in range(subs):
        lines[pl.ds(j, tiles, stride=subs), :] = packed[:, j * LANES : (j + 1) * LANES]
    edges = lines[...].reshape(cols, 2 * own, LANES)
    for r in range(rows):
        first = r % 2 * own
        out_ref[r, :, :own, :] = edges[:, first : first + own, :]
    src_high = jnp.where(live, src // LANES, high)
    src_low = src % LANES
    high_ids = short(lax.broadcasted_iota(jnp.int32, (high, cap), 0))
    low_ids = short(lax.broadcasted_iota(jnp.int32, (LANES, cap), 0))
    total = jnp.zeros((high, LANES), jnp.float32)
    for t in range(tiles):
        total += lax.dot_general(
            equal(high_ids, src_high[t : t + 1]).astype(BITS8),
            equal(low_ids, src_low[t : t + 1]).astype(BITS8),
            NT,
            preferred_element_type=jnp.float32,
        )
    degree = total.astype(jnp.int32)
    for r in range(rows):
        first = r % 2 * (high // 2)
        out_ref[r, :, own:, :] = jnp.broadcast_to(
            degree[first : first + high // 2], (cols, high // 2, LANES)
        )


def ring_col_of(place, cols):
    return 2 * place if place < cols // 2 else 2 * (cols - 1 - place) + 1


def ring_place(col, cols):
    return jnp.where(col % 2 == 0, col // 2, cols - 1 - col // 2)


def ring_col(place, cols):
    return jnp.where(place < cols // 2, 2 * place, 2 * (cols - 1 - place) + 1)


def sum_kernel(cols, shifts, groups, first, last, col_ref, *refs):
    row_ref, *refs = refs
    edge_refs, refs = refs[:2], refs[2:]
    xs, refs = refs[: sum(groups)], refs[sum(groups) :]
    if not first:
        old_ref, old_degree_ref, *refs = refs
    rows, _, depth, _ = edge_refs[0].shape
    out_refs, (counts, scaled, total) = refs[:-3], refs[-3:]
    width = xs[0].shape[1]
    _, sums, src_rows = counts.shape
    highs = src_rows // LOW
    own = depth - src_rows // LANES // 2
    tiles = sums // rows // TILE // 2
    subs = own // tiles
    odd = lax.rem(row_ref[0], 2)
    place = ring_place(col_ref[0], cols)
    blocks = [ring_col(lax.rem(place + shift + cols, cols), cols) for shift in shifts]
    diagonal = lax.broadcasted_iota(jnp.int32, (LANES, LANES), 0) == lax.broadcasted_iota(
        jnp.int32, (LANES, LANES), 1
    )
    target_ids = short(lax.broadcasted_iota(jnp.int32, (TILE, LANES), 0))
    low_ids = short(lax.broadcasted_iota(jnp.int32, (LOW, LANES), 0))

    def as_column(row):
        return jnp.sum(jnp.where(diagonal, row, 0.0), axis=1, keepdims=True)

    def put_scaled(g):
        halves = [
            sum(edge_ref[r, blocks[g], own:, :] for r in range(rows)).astype(jnp.float32)
            for edge_ref in edge_refs
        ]
        degree = jnp.where(odd == 0, jnp.concatenate(halves), jnp.concatenate(halves[::-1]))
        scale = lax.rsqrt(1.0 + degree)
        top = 0
        for x_ref in xs[sum(groups[:g]) : sum(groups[: g + 1])]:
            for i in range(x_ref.shape[0] // LANES):
                column = as_column(scale[top // LANES : top // LANES + 1])
                x = x_ref[i * LANES : (i + 1) * LANES, :].astype(jnp.float32)
                scaled[g % 2, top : top + LANES, :width] = (x * column).astype(jnp.bfloat16)
                top += LANES

    def count_block(g, edge_ref, r, t):
        lefts, rights = [], []
        for j in range(subs):
            edges = edge_ref[r, blocks[g], pl.ds(t * subs + j, 1), :]
            src = edges & 65535
            target_one = equal(target_ids, edges >> 16)
            src_high = src // LOW
            left = [target_one * flag(src_high == h) for h in range(highs)]
            lefts.append(jnp.concatenate(left, axis=0).astype(BITS8))
            rights.append(equal(low_ids, src % LOW).astype(BITS8))
        return lax.dot_general(
            jnp.concatenate(lefts, axis=1),
            jnp.concatenate(rights, axis=1),
            NT,
            preferred_element_type=jnp.float32,
        )

    def add_block(g, convert, unroll, start):
        def fill_tile(part, i, carry):
            block = count_block(g, edge_refs[part], i // tiles, i % tiles)
            top = (part * rows * tiles + i) * TILE
            top = top if unroll else pl.multiple_of(top, TILE)
            for h in range(highs):
                counts[g % 2, pl.ds(top, TILE), h * LOW : (h + 1) * LOW] = convert(
                    block[h * TILE : (h + 1) * TILE]
                )
            return carry

        put_scaled(g)
        for part in range(2):
            if unroll:
                for i in range(rows * tiles):
                    fill_tile(part, i, 0)
            else:
                lax.fori_loop(0, rows * tiles, functools.partial(fill_tile, part), 0)
        added = jnp.dot(counts[g % 2], scaled[g % 2], preferred_element_type=jnp.float32)
        total[...] = added if start else total[...] + added

    scaled[...] = jnp.ones_like(scaled)
    for g in range(len(groups)):
        add_block(g, lambda block: block.astype(jnp.bfloat16), rows * tiles <= 4, g == 0)

    @pl.when(jnp.max(total[:, LANES:]) >= 256.0)
    def _():
        for g in range(len(groups)):
            add_block(
                g,
                lambda block: (block - block.astype(jnp.bfloat16).astype(jnp.float32)).astype(jnp.bfloat16),
                False,
                False,
            )

    if last:
        for shift in range(rows):
            r = lax.rem(row_ref[0] + shift, rows)
            for part in range(2):
                for t in range(tiles):
                    i = (part * rows + r) * tiles + t
                    at = pl.ds(pl.multiple_of(i * TILE, TILE), TILE)
                    value, degree = total[at, :width], total[at, LANES:]
                    if not first:
                        value += old_ref[at, :]
                        degree += as_column(old_degree_ref[pl.ds(i, 1), :])
                    half = 1 - odd if part else odd
                    place = pl.multiple_of((half * tiles + t) * TILE, TILE)
                    norm = lax.rsqrt(1.0 + degree[:, :width])
                    out_refs[shift][pl.ds(place, TILE), :] = (value * norm).astype(jnp.bfloat16)
    else:
        for i in range(sums // TILE):
            at = slice(i * TILE, (i + 1) * TILE)
            line = jnp.sum(jnp.where(diagonal, total[at, LANES:], 0.0), axis=0, keepdims=True)
            value = total[at, :width]
            out_refs[0][at, :] = value if first else value + old_ref[at, :]
            out_refs[1][i : i + 1, :] = line if first else line + old_degree_ref[i : i + 1, :]


def layer_kernel(row_ref, *refs):
    *x_refs, weight_ref, bias_hbm, out_ref, bias, arrived = refs
    copy = pltpu.make_async_copy(bias_hbm, bias, arrived)
    copy.start()
    rows, width = len(x_refs), x_refs[0].shape[1]
    projected = None
    for shift, x_ref in enumerate(x_refs):
        top = pl.multiple_of(lax.rem(row_ref[0] - shift + rows, rows) * width, width)
        part = jnp.dot(x_ref[...], weight_ref[pl.ds(top, width), :], preferred_element_type=jnp.float32)
        projected = part if projected is None else projected + part
    copy.wait()
    out_ref[...] = jnp.maximum(projected + bias[...], 0.0).astype(jnp.bfloat16)


def body(rows, cols, features, weight, bias, edge_src, edge_dst, tile_count):
    tiles, cap = edge_src.shape
    src_rows, width = features.shape
    hidden = weight.shape[1]
    degree_rows = src_rows // LANES
    own_rows = tiles * cap // LANES // cols
    own_nodes = tiles // cols * TILE
    sums = rows * own_nodes
    order = [ring_col_of(place, cols) for place in range(cols)]
    ahead = [(order[p], order[(p + 1) % cols]) for p in range(cols)]
    back = [(order[(p + 1) % cols], order[p]) for p in range(cols)]
    half = src_rows // 2

    depth = (own_rows + degree_rows) // 2
    packed = pl.pallas_call(
        pack_kernel,
        in_specs=[pl.BlockSpec(), pl.BlockSpec(), pl.BlockSpec(memory_space=pltpu.SMEM)],
        out_shape=jax.ShapeDtypeStruct((rows, cols, depth, LANES), jnp.int32),
        scratch_shapes=[pltpu.VMEM((cols * own_rows, LANES), jnp.int32)],
    )(edge_src, edge_dst, tile_count.reshape(tiles))
    edges = lax.all_to_all(
        packed.reshape(rows * cols, depth, LANES),
        ("row", "col"),
        split_axis=0,
        concat_axis=0,
        tiled=True,
    )
    other = lax.ppermute(edges, "row", [(r, r + 1 - 2 * (r % 2)) for r in range(rows)])
    edges = [half.reshape(rows, cols, depth, LANES) for half in (edges, other)]
    col = lax.axis_index("col").astype(jnp.int32).reshape(1)
    row = lax.axis_index("row").astype(jnp.int32).reshape(1)

    smem, vmem = pl.BlockSpec(memory_space=pltpu.SMEM), pl.BlockSpec(memory_space=pltpu.VMEM)

    def add_blocks(total, blocks, last, flops):
        first = total is None
        shifts = [shift for shift, _ in blocks]
        groups = [len(pieces) for _, pieces in blocks]
        pieces = [piece for _, listed in blocks for piece in listed]

        operands = pieces + ([] if first else list(total))
        out_shape = (
            [jax.ShapeDtypeStruct((own_nodes, width), jnp.bfloat16)] * rows
            if last
            else [
                jax.ShapeDtypeStruct((sums, width), jnp.float32),
                jax.ShapeDtypeStruct((sums // TILE, LANES), jnp.float32),
            ]
        )
        scratch = [
            pltpu.VMEM((2, sums, src_rows), jnp.bfloat16),
            pltpu.VMEM((2, src_rows, 2 * LANES), jnp.bfloat16),
            pltpu.VMEM((sums, 2 * LANES), jnp.float32),
        ]
        return pl.pallas_call(
            functools.partial(sum_kernel, cols, shifts, groups, first, last),
            in_specs=[smem] * 2 + [vmem] * (2 + len(operands)),
            out_specs=[vmem] * len(out_shape),
            scratch_shapes=scratch,
            out_shape=out_shape,
            compiler_params=pltpu.CompilerParams(vmem_limit_bytes=48 * 1024 * 1024),
            cost_estimate=pl.CostEstimate(flops=flops, bytes_accessed=2**22, transcendentals=0),
        )(col, row, *edges, *operands)

    block_flops = 2 * sums * src_rows * (2 * LANES + cap)
    ups = downs = features
    total, waiting = None, [(0, [features])]
    for hop in range(1, cols // 2):
        ups = lax.ppermute(ups, "col", ahead)
        downs = lax.ppermute(downs, "col", back)
        waiting += [(-hop, [ups]), (hop, [downs])]
        if hop > 1:
            total = add_blocks(total, waiting, False, 2 * len(waiting) * block_flops)
            waiting = []
    ups = lax.ppermute(ups[:half], "col", ahead)
    downs = lax.ppermute(downs[half:], "col", back)
    waiting.append((cols // 2, [ups, downs]))
    normed = add_blocks(total, waiting, True, block_flops)
    normed = [normed[0]] + [
        lax.ppermute(normed[shift], "row", [(r, (r + shift) % rows) for r in range(rows)])
        for shift in range(1, rows)
    ]
    operands = [*normed, weight]
    return pl.pallas_call(
        layer_kernel,
        grid_spec=pltpu.PrefetchScalarGridSpec(
            num_scalar_prefetch=1,
            grid=(1,),
            in_specs=[pl.BlockSpec(array.shape, lambda i, r: (0, 0)) for array in operands]
            + [pl.BlockSpec(memory_space=pl.ANY)],
            out_specs=pl.BlockSpec((own_nodes, hidden), lambda i, r: (0, 0)),
            scratch_shapes=[pltpu.VMEM((1, hidden), jnp.float32), pltpu.SemaphoreType.DMA],
        ),
        out_shape=jax.ShapeDtypeStruct((own_nodes, hidden), jnp.bfloat16),
        compiler_params=pltpu.CompilerParams(vmem_limit_bytes=8 * 1024 * 1024),
    )(row, *operands, bias.reshape(1, hidden))


def solution(mesh):
    rows, cols = mesh.shape["row"], mesh.shape["col"]
    in_specs = (P("col", "row"), P(), P(), P("row", "col"), P("row", "col"), P("row", "col"))
    out_specs = P(("row", "col"), None)
    return jax.shard_map(
        functools.partial(body, rows, cols),
        mesh=mesh,
        in_specs=in_specs,
        out_specs=out_specs,
        check_vma=False,
    )
```

```python
import functools

import jax
import jax.numpy as jnp
from jax import lax
from jax.experimental import pallas as pl
from jax.experimental.pallas import tpu as pltpu
from jax.sharding import PartitionSpec as P

TILE = 128
LANES = 128
LOW = 256
NT = (((1,), (1,)), ((), ()))
BITS8 = jnp.float8_e4m3fn


def flag(condition):
    return jnp.where(condition, 1.0, 0.0).astype(jnp.bfloat16)


def short(whole):
    return whole.astype(jnp.float32).astype(jnp.bfloat16)


def equal(ids, whole):
    return jnp.where(ids == short(whole), jnp.bfloat16(1), jnp.bfloat16(0))


def pack_kernel(src_ref, dst_ref, count_ref, out_ref, lines):
    tiles, cap = src_ref.shape
    rows, cols, depth, _ = out_ref.shape
    subs = cap // LANES
    own = tiles // cols * subs // 2
    high = 2 * (depth - own)
    src = src_ref[...]
    tile_ids = lax.broadcasted_iota(jnp.int32, (tiles, cap), 0)
    count = jnp.zeros((tiles, cap), jnp.int32)
    for t in range(tiles):
        count = jnp.where(tile_ids == t, count_ref[t], count)
    live = lax.broadcasted_iota(jnp.int32, (tiles, cap), 1) < count
    packed = src + jnp.where(live, dst_ref[...], TILE) * 65536
    for j in range(subs):
        lines[pl.ds(j, tiles, stride=subs), :] = packed[:, j * LANES : (j + 1) * LANES]
    edges = lines[...].reshape(cols, 2 * own, LANES)
    for r in range(rows):
        first = r % 2 * own
        out_ref[r, :, :own, :] = edges[:, first : first + own, :]
    src_high = jnp.where(live, src // LANES, high)
    src_low = src % LANES
    high_ids = short(lax.broadcasted_iota(jnp.int32, (high, cap), 0))
    low_ids = short(lax.broadcasted_iota(jnp.int32, (LANES, cap), 0))
    total = jnp.zeros((high, LANES), jnp.float32)
    for t in range(tiles):
        total += lax.dot_general(
            equal(high_ids, src_high[t : t + 1]).astype(BITS8),
            equal(low_ids, src_low[t : t + 1]).astype(BITS8),
            NT,
            preferred_element_type=jnp.float32,
        )
    degree = total.astype(jnp.int32)
    for r in range(rows):
        first = r % 2 * (high // 2)
        out_ref[r, :, own:, :] = jnp.broadcast_to(
            degree[first : first + high // 2], (cols, high // 2, LANES)
        )


def ring_col_of(place, cols):
    return 2 * place if place < cols // 2 else 2 * (cols - 1 - place) + 1


def ring_place(col, cols):
    return jnp.where(col % 2 == 0, col // 2, cols - 1 - col // 2)


def ring_col(place, cols):
    return jnp.where(place < cols // 2, 2 * place, 2 * (cols - 1 - place) + 1)


def sum_kernel(cols, shifts, groups, first, last, col_ref, *refs):
    row_ref, *refs = refs
    edge_refs, refs = refs[:2], refs[2:]
    xs, refs = refs[: sum(groups)], refs[sum(groups) :]
    if not first:
        old_ref, old_degree_ref, *refs = refs
    rows, _, depth, _ = edge_refs[0].shape
    out_refs, (counts, scaled, total) = refs[:-3], refs[-3:]
    width = xs[0].shape[1]
    _, sums, src_rows = counts.shape
    highs = src_rows // LOW
    own = depth - src_rows // LANES // 2
    tiles = sums // rows // TILE // 2
    subs = own // tiles
    odd = lax.rem(row_ref[0], 2)
    place = ring_place(col_ref[0], cols)
    blocks = [ring_col(lax.rem(place + shift + cols, cols), cols) for shift in shifts]
    diagonal = lax.broadcasted_iota(jnp.int32, (LANES, LANES), 0) == lax.broadcasted_iota(
        jnp.int32, (LANES, LANES), 1
    )
    target_ids = short(lax.broadcasted_iota(jnp.int32, (TILE, LANES), 0))
    low_ids = short(lax.broadcasted_iota(jnp.int32, (LOW, LANES), 0))

    def as_column(row):
        return jnp.sum(jnp.where(diagonal, row, 0.0), axis=1, keepdims=True)

    def put_scaled(g):
        halves = [
            sum(edge_ref[r, blocks[g], own:, :] for r in range(rows)).astype(jnp.float32)
            for edge_ref in edge_refs
        ]
        degree = jnp.where(odd == 0, jnp.concatenate(halves), jnp.concatenate(halves[::-1]))
        scale = lax.rsqrt(1.0 + degree)
        top = 0
        for x_ref in xs[sum(groups[:g]) : sum(groups[: g + 1])]:
            for i in range(x_ref.shape[0] // LANES):
                column = as_column(scale[top // LANES : top // LANES + 1])
                x = x_ref[i * LANES : (i + 1) * LANES, :].astype(jnp.float32)
                scaled[g % 2, top : top + LANES, :width] = (x * column).astype(jnp.bfloat16)
                top += LANES

    def count_block(g, edge_ref, r, t):
        lefts, rights = [], []
        for j in range(subs):
            edges = edge_ref[r, blocks[g], pl.ds(t * subs + j, 1), :]
            src = edges & 65535
            target_one = equal(target_ids, edges >> 16)
            src_high = src // LOW
            left = [target_one * flag(src_high == h) for h in range(highs)]
            lefts.append(jnp.concatenate(left, axis=0).astype(BITS8))
            rights.append(equal(low_ids, src % LOW).astype(BITS8))
        return lax.dot_general(
            jnp.concatenate(lefts, axis=1),
            jnp.concatenate(rights, axis=1),
            NT,
            preferred_element_type=jnp.float32,
        )

    def add_block(g, convert, unroll, start):
        def fill_tile(part, i, carry):
            block = count_block(g, edge_refs[part], i // tiles, i % tiles)
            top = (part * rows * tiles + i) * TILE
            top = top if unroll else pl.multiple_of(top, TILE)
            for h in range(highs):
                counts[g % 2, pl.ds(top, TILE), h * LOW : (h + 1) * LOW] = convert(
                    block[h * TILE : (h + 1) * TILE]
                )
            return carry

        put_scaled(g)
        for part in range(2):
            if unroll:
                for i in range(rows * tiles):
                    fill_tile(part, i, 0)
            else:
                lax.fori_loop(0, rows * tiles, functools.partial(fill_tile, part), 0)
        added = jnp.dot(counts[g % 2], scaled[g % 2], preferred_element_type=jnp.float32)
        total[...] = added if start else total[...] + added

    scaled[...] = jnp.ones_like(scaled)
    for g in range(len(groups)):
        add_block(g, lambda block: block.astype(jnp.bfloat16), rows * tiles <= 4, g == 0)

    @pl.when(jnp.max(total[:, LANES:]) >= 256.0)
    def _():
        for g in range(len(groups)):
            add_block(
                g,
                lambda block: (block - block.astype(jnp.bfloat16).astype(jnp.float32)).astype(jnp.bfloat16),
                False,
                False,
            )

    if last:
        for shift in range(rows):
            r = lax.rem(row_ref[0] + shift, rows)
            for part in range(2):
                for t in range(tiles):
                    i = (part * rows + r) * tiles + t
                    at = pl.ds(pl.multiple_of(i * TILE, TILE), TILE)
                    value, degree = total[at, :width], total[at, LANES:]
                    if not first:
                        value += old_ref[at, :]
                        degree += as_column(old_degree_ref[pl.ds(i, 1), :])
                    half = 1 - odd if part else odd
                    place = pl.multiple_of((half * tiles + t) * TILE, TILE)
                    norm = lax.rsqrt(1.0 + degree[:, :width])
                    out_refs[shift][pl.ds(place, TILE), :] = (value * norm).astype(jnp.bfloat16)
    else:
        for i in range(sums // TILE):
            at = slice(i * TILE, (i + 1) * TILE)
            line = jnp.sum(jnp.where(diagonal, total[at, LANES:], 0.0), axis=0, keepdims=True)
            value = total[at, :width]
            out_refs[0][at, :] = value if first else value + old_ref[at, :]
            out_refs[1][i : i + 1, :] = line if first else line + old_degree_ref[i : i + 1, :]


def layer_kernel(row_ref, *refs):
    *x_refs, weight_ref, bias_hbm, out_ref, bias, arrived = refs
    copy = pltpu.make_async_copy(bias_hbm, bias, arrived)
    copy.start()
    rows, width = len(x_refs), x_refs[0].shape[1]
    projected = None
    for shift, x_ref in enumerate(x_refs):
        top = pl.multiple_of(lax.rem(row_ref[0] - shift + rows, rows) * width, width)
        part = jnp.dot(x_ref[...], weight_ref[pl.ds(top, width), :], preferred_element_type=jnp.float32)
        projected = part if projected is None else projected + part
    copy.wait()
    out_ref[...] = jnp.maximum(projected + bias[...], 0.0).astype(jnp.bfloat16)


def body(rows, cols, features, weight, bias, edge_src, edge_dst, tile_count):
    tiles, cap = edge_src.shape
    src_rows, width = features.shape
    hidden = weight.shape[1]
    degree_rows = src_rows // LANES
    own_rows = tiles * cap // LANES // cols
    own_nodes = tiles // cols * TILE
    sums = rows * own_nodes
    order = [ring_col_of(place, cols) for place in range(cols)]
    ahead = [(order[p], order[(p + 1) % cols]) for p in range(cols)]
    back = [(order[(p + 1) % cols], order[p]) for p in range(cols)]
    half = src_rows // 2

    depth = (own_rows + degree_rows) // 2
    packed = pl.pallas_call(
        pack_kernel,
        in_specs=[pl.BlockSpec(), pl.BlockSpec(), pl.BlockSpec(memory_space=pltpu.SMEM)],
        out_shape=jax.ShapeDtypeStruct((rows, cols, depth, LANES), jnp.int32),
        scratch_shapes=[pltpu.VMEM((cols * own_rows, LANES), jnp.int32)],
    )(edge_src, edge_dst, tile_count.reshape(tiles))
    edges = lax.all_to_all(
        packed.reshape(rows * cols, depth, LANES),
        ("row", "col"),
        split_axis=0,
        concat_axis=0,
        tiled=True,
    )
    other = lax.ppermute(edges, "row", [(r, r + 1 - 2 * (r % 2)) for r in range(rows)])
    edges = [half.reshape(rows, cols, depth, LANES) for half in (edges, other)]
    col = lax.axis_index("col").astype(jnp.int32).reshape(1)
    row = lax.axis_index("row").astype(jnp.int32).reshape(1)

    smem, vmem = pl.BlockSpec(memory_space=pltpu.SMEM), pl.BlockSpec(memory_space=pltpu.VMEM)

    def add_blocks(total, blocks, last, flops):
        first = total is None
        shifts = [shift for shift, _ in blocks]
        groups = [len(pieces) for _, pieces in blocks]
        pieces = [piece for _, listed in blocks for piece in listed]

        operands = pieces + ([] if first else list(total))
        out_shape = (
            [pltpu.VMEM((own_nodes, width), jnp.bfloat16)] * rows
            if last
            else [
                pltpu.VMEM((sums, width), jnp.float32),
                pltpu.VMEM((sums // TILE, LANES), jnp.float32),
            ]
        )
        scratch = [
            pltpu.VMEM((2, sums, src_rows), jnp.bfloat16),
            pltpu.VMEM((2, src_rows, 2 * LANES), jnp.bfloat16),
            pltpu.VMEM((sums, 2 * LANES), jnp.float32),
        ]
        return pl.pallas_call(
            functools.partial(sum_kernel, cols, shifts, groups, first, last),
            in_specs=[smem] * 2 + [vmem] * (2 + len(operands)),
            out_specs=[vmem] * len(out_shape),
            scratch_shapes=scratch,
            out_shape=out_shape,
            compiler_params=pltpu.CompilerParams(vmem_limit_bytes=48 * 1024 * 1024),
            cost_estimate=pl.CostEstimate(flops=flops, bytes_accessed=2**22, transcendentals=0),
        )(col, row, *[pltpu.with_memory_space_constraint(array, pltpu.VMEM) for array in edges + operands])

    block_flops = 2 * sums * src_rows * (2 * LANES + cap)
    ups = downs = features
    total, waiting = None, [(0, [features])]
    for hop in range(1, cols // 2):
        ups = lax.ppermute(ups, "col", ahead)
        downs = lax.ppermute(downs, "col", back)
        waiting += [(-hop, [ups]), (hop, [downs])]
        if hop > 1:
            total = add_blocks(total, waiting, False, 2 * len(waiting) * block_flops)
            waiting = []
    ups = lax.ppermute(ups[:half], "col", ahead)
    downs = lax.ppermute(downs[half:], "col", back)
    waiting.append((cols // 2, [ups, downs]))
    normed = add_blocks(total, waiting, True, block_flops)
    normed = [normed[0]] + [
        lax.ppermute(normed[shift], "row", [(r, (r + shift) % rows) for r in range(rows)])
        for shift in range(1, rows)
    ]
    operands = [*normed, weight]
    return pl.pallas_call(
        layer_kernel,
        grid_spec=pltpu.PrefetchScalarGridSpec(
            num_scalar_prefetch=1,
            grid=(1,),
            in_specs=[pl.BlockSpec(array.shape, lambda i, r: (0, 0)) for array in operands]
            + [pl.BlockSpec(memory_space=pl.ANY)],
            out_specs=pl.BlockSpec((own_nodes, hidden), lambda i, r: (0, 0)),
            scratch_shapes=[pltpu.VMEM((1, hidden), jnp.float32), pltpu.SemaphoreType.DMA],
        ),
        out_shape=jax.ShapeDtypeStruct((own_nodes, hidden), jnp.bfloat16),
        compiler_params=pltpu.CompilerParams(vmem_limit_bytes=8 * 1024 * 1024),
    )(row, *operands, bias.reshape(1, hidden))


def solution(mesh):
    rows, cols = mesh.shape["row"], mesh.shape["col"]
    in_specs = (P("col", "row"), P(), P(), P("row", "col"), P("row", "col"), P("row", "col"))
    out_specs = P(("row", "col"), None)
    return jax.shard_map(
        functools.partial(body, rows, cols),
        mesh=mesh,
        in_specs=in_specs,
        out_specs=out_specs,
        check_vma=False,
    )
```

```python
import functools

import jax
import jax.numpy as jnp
from jax import lax
from jax.experimental import pallas as pl
from jax.experimental.pallas import tpu as pltpu
from jax.sharding import PartitionSpec as P

TILE = 128
LANES = 128
LOW = 256
NT = (((1,), (1,)), ((), ()))
BITS8 = jnp.float8_e4m3fn


def flag(condition):
    return jnp.where(condition, 1.0, 0.0).astype(jnp.bfloat16)


def short(whole):
    return whole.astype(jnp.float32).astype(jnp.bfloat16)


def equal(ids, whole):
    return jnp.where(ids == short(whole), jnp.bfloat16(1), jnp.bfloat16(0))


def pack_kernel(src_ref, dst_ref, count_ref, out_ref, lines):
    tiles, cap = src_ref.shape
    rows, cols, depth, _ = out_ref.shape
    subs = cap // LANES
    own = tiles // cols * subs // 2
    high = 2 * (depth - own)
    src = src_ref[...]
    tile_ids = lax.broadcasted_iota(jnp.int32, (tiles, cap), 0)
    count = jnp.zeros((tiles, cap), jnp.int32)
    for t in range(tiles):
        count = jnp.where(tile_ids == t, count_ref[t], count)
    live = lax.broadcasted_iota(jnp.int32, (tiles, cap), 1) < count
    packed = src + jnp.where(live, dst_ref[...], TILE) * 65536
    for j in range(subs):
        lines[pl.ds(j, tiles, stride=subs), :] = packed[:, j * LANES : (j + 1) * LANES]
    edges = lines[...].reshape(cols, 2 * own, LANES)
    for r in range(rows):
        first = r % 2 * own
        out_ref[r, :, :own, :] = edges[:, first : first + own, :]
    src_high = jnp.where(live, src // LANES, high)
    src_low = src % LANES
    high_ids = short(lax.broadcasted_iota(jnp.int32, (high, cap), 0))
    low_ids = short(lax.broadcasted_iota(jnp.int32, (LANES, cap), 0))
    total = jnp.zeros((high, LANES), jnp.float32)
    for t in range(tiles):
        total += lax.dot_general(
            equal(high_ids, src_high[t : t + 1]).astype(BITS8),
            equal(low_ids, src_low[t : t + 1]).astype(BITS8),
            NT,
            preferred_element_type=jnp.float32,
        )
    degree = total.astype(jnp.int32)
    for r in range(rows):
        first = r % 2 * (high // 2)
        out_ref[r, :, own:, :] = jnp.broadcast_to(
            degree[first : first + high // 2], (cols, high // 2, LANES)
        )


def ring_col_of(place, cols):
    return 2 * place if place < cols // 2 else 2 * (cols - 1 - place) + 1


def ring_place(col, cols):
    return jnp.where(col % 2 == 0, col // 2, cols - 1 - col // 2)


def ring_col(place, cols):
    return jnp.where(place < cols // 2, 2 * place, 2 * (cols - 1 - place) + 1)


def sum_kernel(cols, shifts, groups, first, last, col_ref, *refs):
    row_ref, *refs = refs
    edge_refs, refs = refs[:2], refs[2:]
    xs, refs = refs[: sum(groups)], refs[sum(groups) :]
    if not first:
        old_ref, old_degree_ref, *refs = refs
    rows, _, depth, _ = edge_refs[0].shape
    out_refs, (counts, scaled, total) = refs[:-3], refs[-3:]
    width = xs[0].shape[1]
    sums, src_rows = counts.shape
    highs = src_rows // LOW
    own = depth - src_rows // LANES // 2
    tiles = sums // rows // TILE // 2
    subs = own // tiles
    odd = lax.rem(row_ref[0], 2)
    place = ring_place(col_ref[0], cols)
    diagonal = lax.broadcasted_iota(jnp.int32, (LANES, LANES), 0) == lax.broadcasted_iota(
        jnp.int32, (LANES, LANES), 1
    )
    target_ids = short(lax.broadcasted_iota(jnp.int32, (TILE, LANES), 0))
    low_ids = short(lax.broadcasted_iota(jnp.int32, (LOW, LANES), 0))

    def as_column(row):
        return jnp.sum(jnp.where(diagonal, row, 0.0), axis=1, keepdims=True)

    def put_scaled(block, pieces):
        halves = [
            sum(edge_ref[r, block, own:, :] for r in range(rows)).astype(jnp.float32)
            for edge_ref in edge_refs
        ]
        degree = jnp.where(odd == 0, jnp.concatenate(halves), jnp.concatenate(halves[::-1]))
        scale = lax.rsqrt(1.0 + degree)
        top = 0
        for x_ref in pieces:
            for i in range(x_ref.shape[0] // LANES):
                column = as_column(scale[top // LANES : top // LANES + 1])
                x = x_ref[i * LANES : (i + 1) * LANES, :].astype(jnp.float32)
                scaled[top : top + LANES, :width] = (x * column).astype(jnp.bfloat16)
                top += LANES

    def count_block(block, edge_ref, r, t):
        lefts, rights = [], []
        for j in range(subs):
            edges = edge_ref[r, block, pl.ds(t * subs + j, 1), :]
            src = edges & 65535
            target_one = equal(target_ids, edges >> 16)
            src_high = src // LOW
            left = [target_one * flag(src_high == h) for h in range(highs)]
            lefts.append(jnp.concatenate(left, axis=0).astype(BITS8))
            rights.append(equal(low_ids, src % LOW).astype(BITS8))
        return lax.dot_general(
            jnp.concatenate(lefts, axis=1),
            jnp.concatenate(rights, axis=1),
            NT,
            preferred_element_type=jnp.float32,
        )

    def add_block(convert, unroll, g, carry):
        ahead = shifts[0]
        for k in range(1, len(shifts)):
            ahead = jnp.where(g == k, shifts[k], ahead)
        block = ring_col(lax.rem(place + ahead + cols, cols), cols)

        def fill_tile(part, i, carry):
            tile = count_block(block, edge_refs[part], i // tiles, i % tiles)
            top = (part * rows * tiles + i) * TILE
            top = top if unroll else pl.multiple_of(top, TILE)
            for h in range(highs):
                counts[pl.ds(top, TILE), h * LOW : (h + 1) * LOW] = convert(
                    tile[h * TILE : (h + 1) * TILE]
                )
            return carry

        for k in range(len(groups)):
            pieces = xs[sum(groups[:k]) : sum(groups[: k + 1])]
            pl.when(g == k)(functools.partial(put_scaled, block, pieces))
        for part in range(2):
            if unroll:
                for i in range(rows * tiles):
                    fill_tile(part, i, 0)
            else:
                lax.fori_loop(0, rows * tiles, functools.partial(fill_tile, part), 0)
        total[...] += jnp.dot(counts[...], scaled[...], preferred_element_type=jnp.float32)
        return carry

    def rounded(tile):
        return tile.astype(jnp.bfloat16)

    def remainder(tile):
        return (tile - tile.astype(jnp.bfloat16).astype(jnp.float32)).astype(jnp.bfloat16)

    scaled[...] = jnp.ones_like(scaled)
    total[...] = jnp.zeros_like(total)
    lax.fori_loop(0, len(groups), functools.partial(add_block, rounded, rows * tiles <= 4), 0)

    @pl.when(jnp.max(total[:, LANES:]) >= 256.0)
    def _():
        lax.fori_loop(0, len(groups), functools.partial(add_block, remainder, False), 0)

    if last:
        for shift in range(rows):
            r = lax.rem(row_ref[0] + shift, rows)
            for part in range(2):
                for t in range(tiles):
                    i = (part * rows + r) * tiles + t
                    at = pl.ds(pl.multiple_of(i * TILE, TILE), TILE)
                    value, degree = total[at, :width], total[at, LANES:]
                    if not first:
                        value += old_ref[at, :]
                        degree += as_column(old_degree_ref[pl.ds(i, 1), :])
                    half = 1 - odd if part else odd
                    place = pl.multiple_of((half * tiles + t) * TILE, TILE)
                    norm = lax.rsqrt(1.0 + degree[:, :width])
                    out_refs[shift][pl.ds(place, TILE), :] = (value * norm).astype(jnp.bfloat16)
    else:
        for i in range(sums // TILE):
            at = slice(i * TILE, (i + 1) * TILE)
            line = jnp.sum(jnp.where(diagonal, total[at, LANES:], 0.0), axis=0, keepdims=True)
            value = total[at, :width]
            out_refs[0][at, :] = value if first else value + old_ref[at, :]
            out_refs[1][i : i + 1, :] = line if first else line + old_degree_ref[i : i + 1, :]


def layer_kernel(row_ref, *refs):
    *x_refs, weight_ref, bias_hbm, out_ref, bias, arrived = refs
    copy = pltpu.make_async_copy(bias_hbm, bias, arrived)
    copy.start()
    rows, width = len(x_refs), x_refs[0].shape[1]
    projected = None
    for shift, x_ref in enumerate(x_refs):
        top = pl.multiple_of(lax.rem(row_ref[0] - shift + rows, rows) * width, width)
        part = jnp.dot(x_ref[...], weight_ref[pl.ds(top, width), :], preferred_element_type=jnp.float32)
        projected = part if projected is None else projected + part
    copy.wait()
    out_ref[...] = jnp.maximum(projected + bias[...], 0.0).astype(jnp.bfloat16)


def body(rows, cols, features, weight, bias, edge_src, edge_dst, tile_count):
    tiles, cap = edge_src.shape
    src_rows, width = features.shape
    hidden = weight.shape[1]
    degree_rows = src_rows // LANES
    own_rows = tiles * cap // LANES // cols
    own_nodes = tiles // cols * TILE
    sums = rows * own_nodes
    order = [ring_col_of(place, cols) for place in range(cols)]
    ahead = [(order[p], order[(p + 1) % cols]) for p in range(cols)]
    back = [(order[(p + 1) % cols], order[p]) for p in range(cols)]
    half = src_rows // 2

    depth = (own_rows + degree_rows) // 2
    packed = pl.pallas_call(
        pack_kernel,
        in_specs=[pl.BlockSpec(), pl.BlockSpec(), pl.BlockSpec(memory_space=pltpu.SMEM)],
        out_shape=jax.ShapeDtypeStruct((rows, cols, depth, LANES), jnp.int32),
        scratch_shapes=[pltpu.VMEM((cols * own_rows, LANES), jnp.int32)],
    )(edge_src, edge_dst, tile_count.reshape(tiles))
    edges = lax.all_to_all(
        packed.reshape(rows * cols, depth, LANES),
        ("row", "col"),
        split_axis=0,
        concat_axis=0,
        tiled=True,
    )
    other = lax.ppermute(edges, "row", [(r, r + 1 - 2 * (r % 2)) for r in range(rows)])
    edges = [half.reshape(rows, cols, depth, LANES) for half in (edges, other)]
    col = lax.axis_index("col").astype(jnp.int32).reshape(1)
    row = lax.axis_index("row").astype(jnp.int32).reshape(1)

    smem, vmem = pl.BlockSpec(memory_space=pltpu.SMEM), pl.BlockSpec(memory_space=pltpu.VMEM)

    def add_blocks(total, blocks, last, flops):
        first = total is None
        shifts = [shift for shift, _ in blocks]
        groups = [len(pieces) for _, pieces in blocks]
        pieces = [piece for _, listed in blocks for piece in listed]

        operands = pieces + ([] if first else list(total))
        out_shape = (
            [jax.ShapeDtypeStruct((own_nodes, width), jnp.bfloat16)] * rows
            if last
            else [
                jax.ShapeDtypeStruct((sums, width), jnp.float32),
                jax.ShapeDtypeStruct((sums // TILE, LANES), jnp.float32),
            ]
        )
        scratch = [
            pltpu.VMEM((sums, src_rows), jnp.bfloat16),
            pltpu.VMEM((src_rows, 2 * LANES), jnp.bfloat16),
            pltpu.VMEM((sums, 2 * LANES), jnp.float32),
        ]
        return pl.pallas_call(
            functools.partial(sum_kernel, cols, shifts, groups, first, last),
            in_specs=[smem] * 2 + [vmem] * (2 + len(operands)),
            out_specs=[vmem] * len(out_shape),
            scratch_shapes=scratch,
            out_shape=out_shape,
            compiler_params=pltpu.CompilerParams(vmem_limit_bytes=48 * 1024 * 1024),
            cost_estimate=pl.CostEstimate(flops=flops, bytes_accessed=2**22, transcendentals=0),
        )(col, row, *edges, *operands)

    block_flops = 2 * sums * src_rows * (2 * LANES + cap)
    ups = downs = features
    total, waiting = None, [(0, [features])]
    for hop in range(1, cols // 2):
        ups = lax.ppermute(ups, "col", ahead)
        downs = lax.ppermute(downs, "col", back)
        waiting += [(-hop, [ups]), (hop, [downs])]
        if hop > 1:
            total = add_blocks(total, waiting, False, 2 * len(waiting) * block_flops)
            waiting = []
    ups = lax.ppermute(ups[:half], "col", ahead)
    downs = lax.ppermute(downs[half:], "col", back)
    waiting.append((cols // 2, [ups, downs]))
    normed = add_blocks(total, waiting, True, block_flops)
    normed = [normed[0]] + [
        lax.ppermute(normed[shift], "row", [(r, (r + shift) % rows) for r in range(rows)])
        for shift in range(1, rows)
    ]
    operands = [*normed, weight]
    return pl.pallas_call(
        layer_kernel,
        grid_spec=pltpu.PrefetchScalarGridSpec(
            num_scalar_prefetch=1,
            grid=(1,),
            in_specs=[pl.BlockSpec(array.shape, lambda i, r: (0, 0)) for array in operands]
            + [pl.BlockSpec(memory_space=pl.ANY)],
            out_specs=pl.BlockSpec((own_nodes, hidden), lambda i, r: (0, 0)),
            scratch_shapes=[pltpu.VMEM((1, hidden), jnp.float32), pltpu.SemaphoreType.DMA],
        ),
        out_shape=jax.ShapeDtypeStruct((own_nodes, hidden), jnp.bfloat16),
        compiler_params=pltpu.CompilerParams(vmem_limit_bytes=8 * 1024 * 1024),
    )(row, *operands, bias.reshape(1, hidden))


def solution(mesh):
    rows, cols = mesh.shape["row"], mesh.shape["col"]
    in_specs = (P("col", "row"), P(), P(), P("row", "col"), P("row", "col"), P("row", "col"))
    out_specs = P(("row", "col"), None)
    return jax.shard_map(
        functools.partial(body, rows, cols),
        mesh=mesh,
        in_specs=in_specs,
        out_specs=out_specs,
        check_vma=False,
    )
```

```python
import functools

import jax
import jax.numpy as jnp
from jax import lax
from jax.experimental import pallas as pl
from jax.experimental.pallas import tpu as pltpu
from jax.sharding import PartitionSpec as P

TILE = 128
LANES = 128
LOW = 256
NT = (((1,), (1,)), ((), ()))
BITS8 = jnp.float8_e4m3fn


def flag(condition):
    return jnp.where(condition, 1.0, 0.0).astype(jnp.bfloat16)


def short(whole):
    return whole.astype(jnp.float32).astype(jnp.bfloat16)


def equal(ids, whole):
    return jnp.where(ids == short(whole), jnp.bfloat16(1), jnp.bfloat16(0))


def pack_kernel(src_ref, dst_ref, count_ref, out_ref, lines):
    tiles, cap = src_ref.shape
    rows, cols, depth, _ = out_ref.shape
    subs = cap // LANES
    own = tiles // cols * subs // 2
    high = 2 * (depth - own)
    src = src_ref[...]
    tile_ids = lax.broadcasted_iota(jnp.int32, (tiles, cap), 0)
    count = jnp.zeros((tiles, cap), jnp.int32)
    for t in range(tiles):
        count = jnp.where(tile_ids == t, count_ref[t], count)
    live = lax.broadcasted_iota(jnp.int32, (tiles, cap), 1) < count
    packed = src + jnp.where(live, dst_ref[...], TILE) * 65536
    for j in range(subs):
        lines[pl.ds(j, tiles, stride=subs), :] = packed[:, j * LANES : (j + 1) * LANES]
    edges = lines[...].reshape(cols, 2 * own, LANES)
    for r in range(rows):
        first = r % 2 * own
        out_ref[r, :, :own, :] = edges[:, first : first + own, :]
    src_high = jnp.where(live, src // LANES, high)
    src_low = src % LANES
    high_ids = short(lax.broadcasted_iota(jnp.int32, (high, cap), 0))
    low_ids = short(lax.broadcasted_iota(jnp.int32, (LANES, cap), 0))
    total = jnp.zeros((high, LANES), jnp.float32)
    for t in range(tiles):
        total += lax.dot_general(
            equal(high_ids, src_high[t : t + 1]).astype(BITS8),
            equal(low_ids, src_low[t : t + 1]).astype(BITS8),
            NT,
            preferred_element_type=jnp.float32,
        )
    degree = total.astype(jnp.int32)
    for r in range(rows):
        first = r % 2 * (high // 2)
        out_ref[r, :, own:, :] = jnp.broadcast_to(
            degree[first : first + high // 2], (cols, high // 2, LANES)
        )


def ring_col_of(place, cols):
    return 2 * place if place < cols // 2 else 2 * (cols - 1 - place) + 1


def ring_place(col, cols):
    return jnp.where(col % 2 == 0, col // 2, cols - 1 - col // 2)


def ring_col(place, cols):
    return jnp.where(place < cols // 2, 2 * place, 2 * (cols - 1 - place) + 1)


def sum_kernel(cols, shifts, groups, first, last, col_ref, *refs):
    row_ref, *refs = refs
    edge_refs, refs = refs[:2], refs[2:]
    xs, refs = refs[: sum(groups)], refs[sum(groups) :]
    if not first:
        old_ref, old_degree_ref, *refs = refs
    rows, _, depth, _ = edge_refs[0].shape
    out_refs, (counts, scaled, total) = refs[:-3], refs[-3:]
    width = xs[0].shape[1]
    _, sums, src_rows = counts.shape
    highs = src_rows // LOW
    own = depth - src_rows // LANES // 2
    tiles = sums // rows // TILE // 2
    subs = own // tiles
    odd = lax.rem(row_ref[0], 2)
    place = ring_place(col_ref[0], cols)
    sign = 1 - 2 * lax.rem(place, 2)
    blocks = [ring_col(lax.rem(place + sign * shift + cols, cols), cols) for shift in shifts]
    diagonal = lax.broadcasted_iota(jnp.int32, (LANES, LANES), 0) == lax.broadcasted_iota(
        jnp.int32, (LANES, LANES), 1
    )
    target_ids = short(lax.broadcasted_iota(jnp.int32, (TILE, LANES), 0))
    low_ids = short(lax.broadcasted_iota(jnp.int32, (LOW, LANES), 0))

    def as_column(row):
        return jnp.sum(jnp.where(diagonal, row, 0.0), axis=1, keepdims=True)

    def put_scaled(g):
        halves = [
            sum(edge_ref[r, blocks[g], own:, :] for r in range(rows)).astype(jnp.float32)
            for edge_ref in edge_refs
        ]
        degree = jnp.where(odd == 0, jnp.concatenate(halves), jnp.concatenate(halves[::-1]))
        scale = lax.rsqrt(1.0 + degree)
        top = 0
        for x_ref in xs[sum(groups[:g]) : sum(groups[: g + 1])]:
            for i in range(x_ref.shape[0] // LANES):
                column = as_column(scale[top // LANES : top // LANES + 1])
                x = x_ref[i * LANES : (i + 1) * LANES, :].astype(jnp.float32)
                scaled[g % 2, top : top + LANES, :width] = (x * column).astype(jnp.bfloat16)
                top += LANES

    def count_block(g, edge_ref, r, t):
        lefts, rights = [], []
        for j in range(subs):
            edges = edge_ref[r, blocks[g], pl.ds(t * subs + j, 1), :]
            src = edges & 65535
            target_one = equal(target_ids, edges >> 16)
            src_high = src // LOW
            left = [target_one * flag(src_high == h) for h in range(highs)]
            lefts.append(jnp.concatenate(left, axis=0).astype(BITS8))
            rights.append(equal(low_ids, src % LOW).astype(BITS8))
        return lax.dot_general(
            jnp.concatenate(lefts, axis=1),
            jnp.concatenate(rights, axis=1),
            NT,
            preferred_element_type=jnp.float32,
        )

    def add_block(g, convert, unroll, start):
        def fill_tile(part, i, carry):
            block = count_block(g, edge_refs[part], i // tiles, i % tiles)
            top = (part * rows * tiles + i) * TILE
            top = top if unroll else pl.multiple_of(top, TILE)
            for h in range(highs):
                counts[g % 2, pl.ds(top, TILE), h * LOW : (h + 1) * LOW] = convert(
                    block[h * TILE : (h + 1) * TILE]
                )
            return carry

        put_scaled(g)
        for part in range(2):
            if unroll:
                for i in range(rows * tiles):
                    fill_tile(part, i, 0)
            else:
                lax.fori_loop(0, rows * tiles, functools.partial(fill_tile, part), 0)
        added = jnp.dot(counts[g % 2], scaled[g % 2], preferred_element_type=jnp.float32)
        total[...] = added if start else total[...] + added

    scaled[...] = jnp.ones_like(scaled)
    for g in range(len(groups)):
        add_block(g, lambda block: block.astype(jnp.bfloat16), rows * tiles <= 4, g == 0)

    @pl.when(jnp.max(total[:, LANES:]) >= 256.0)
    def _():
        for g in range(len(groups)):
            add_block(
                g,
                lambda block: (block - block.astype(jnp.bfloat16).astype(jnp.float32)).astype(jnp.bfloat16),
                False,
                False,
            )

    if last:
        for shift in range(rows):
            r = row_ref[0] ^ shift
            for part in range(2):
                for t in range(tiles):
                    i = (part * rows + r) * tiles + t
                    at = pl.ds(pl.multiple_of(i * TILE, TILE), TILE)
                    value, degree = total[at, :width], total[at, LANES:]
                    if not first:
                        value += old_ref[at, :]
                        degree += as_column(old_degree_ref[pl.ds(i, 1), :])
                    half = 1 - odd if part else odd
                    place = pl.multiple_of((half * tiles + t) * TILE, TILE)
                    norm = lax.rsqrt(1.0 + degree[:, :width])
                    out_refs[shift][pl.ds(place, TILE), :] = (value * norm).astype(jnp.bfloat16)
    else:
        for i in range(sums // TILE):
            at = slice(i * TILE, (i + 1) * TILE)
            line = jnp.sum(jnp.where(diagonal, total[at, LANES:], 0.0), axis=0, keepdims=True)
            value = total[at, :width]
            out_refs[0][at, :] = value if first else value + old_ref[at, :]
            out_refs[1][i : i + 1, :] = line if first else line + old_degree_ref[i : i + 1, :]


def layer_kernel(row_ref, *refs):
    *x_refs, weight_ref, bias_hbm, out_ref, bias, arrived = refs
    copy = pltpu.make_async_copy(bias_hbm, bias, arrived)
    copy.start()
    rows, width = len(x_refs), x_refs[0].shape[1]
    projected = None
    for shift, x_ref in enumerate(x_refs):
        top = pl.multiple_of((row_ref[0] ^ shift) * width, width)
        part = jnp.dot(x_ref[...], weight_ref[pl.ds(top, width), :], preferred_element_type=jnp.float32)
        projected = part if projected is None else projected + part
    copy.wait()
    out_ref[...] = jnp.maximum(projected + bias[...], 0.0).astype(jnp.bfloat16)


def body(rows, cols, features, weight, bias, edge_src, edge_dst, tile_count):
    tiles, cap = edge_src.shape
    src_rows, width = features.shape
    hidden = weight.shape[1]
    degree_rows = src_rows // LANES
    own_rows = tiles * cap // LANES // cols
    own_nodes = tiles // cols * TILE
    sums = rows * own_nodes
    order = [ring_col_of(place, cols) for place in range(cols)]
    near = [(order[p], order[p ^ 1]) for p in range(cols)]
    next_near = [(order[p], order[((p + 1) % cols ^ 1) - 1]) for p in range(cols)]
    half = src_rows // 2

    depth = (own_rows + degree_rows) // 2
    packed = pl.pallas_call(
        pack_kernel,
        in_specs=[pl.BlockSpec(), pl.BlockSpec(), pl.BlockSpec(memory_space=pltpu.SMEM)],
        out_shape=jax.ShapeDtypeStruct((rows, cols, depth, LANES), jnp.int32),
        scratch_shapes=[pltpu.VMEM((cols * own_rows, LANES), jnp.int32)],
    )(edge_src, edge_dst, tile_count.reshape(tiles))
    edges = lax.all_to_all(
        packed.reshape(rows * cols, depth, LANES),
        ("row", "col"),
        split_axis=0,
        concat_axis=0,
        tiled=True,
    )
    other = lax.ppermute(edges, "row", [(r, r ^ 1) for r in range(rows)])
    edges = [half.reshape(rows, cols, depth, LANES) for half in (edges, other)]
    col = lax.axis_index("col").astype(jnp.int32).reshape(1)
    row = lax.axis_index("row").astype(jnp.int32).reshape(1)

    smem, vmem = pl.BlockSpec(memory_space=pltpu.SMEM), pl.BlockSpec(memory_space=pltpu.VMEM)

    def add_blocks(total, blocks, last, flops):
        first = total is None
        shifts = [shift for shift, _ in blocks]
        groups = [len(pieces) for _, pieces in blocks]
        pieces = [piece for _, listed in blocks for piece in listed]

        operands = pieces + ([] if first else list(total))
        out_shape = (
            [jax.ShapeDtypeStruct((own_nodes, width), jnp.bfloat16)] * rows
            if last
            else [
                jax.ShapeDtypeStruct((sums, width), jnp.float32),
                jax.ShapeDtypeStruct((sums // TILE, LANES), jnp.float32),
            ]
        )
        scratch = [
            pltpu.VMEM((2, sums, src_rows), jnp.bfloat16),
            pltpu.VMEM((2, src_rows, 2 * LANES), jnp.bfloat16),
            pltpu.VMEM((sums, 2 * LANES), jnp.float32),
        ]
        return pl.pallas_call(
            functools.partial(sum_kernel, cols, shifts, groups, first, last),
            in_specs=[smem] * 2 + [vmem] * (2 + len(operands)),
            out_specs=[vmem] * len(out_shape),
            scratch_shapes=scratch,
            out_shape=out_shape,
            compiler_params=pltpu.CompilerParams(vmem_limit_bytes=48 * 1024 * 1024),
            cost_estimate=pl.CostEstimate(flops=flops, bytes_accessed=2**22, transcendentals=0),
        )(col, row, *edges, *operands)

    block_flops = 2 * sums * src_rows * (2 * LANES + cap)
    here = there = features
    total, waiting = None, [(0, [features])]
    for hop in range(1, cols // 2):
        here, there = lax.ppermute(there, "col", near), lax.ppermute(here, "col", next_near)
        waiting += [(hop, [here]), (-hop, [there])]
        if hop > 1:
            total = add_blocks(total, waiting, False, 2 * len(waiting) * block_flops)
            waiting = []
    upper = lax.ppermute(there[:half], "col", near)
    lower = lax.ppermute(here[half:], "col", next_near)
    waiting.append((cols // 2, [upper, lower]))
    normed = add_blocks(total, waiting, True, block_flops)
    normed = [normed[0]] + [
        lax.ppermute(normed[shift], "row", [(r, r ^ shift) for r in range(rows)])
        for shift in range(1, rows)
    ]
    operands = [*normed, weight]
    return pl.pallas_call(
        layer_kernel,
        grid_spec=pltpu.PrefetchScalarGridSpec(
            num_scalar_prefetch=1,
            grid=(1,),
            in_specs=[pl.BlockSpec(array.shape, lambda i, r: (0, 0)) for array in operands]
            + [pl.BlockSpec(memory_space=pl.ANY)],
            out_specs=pl.BlockSpec((own_nodes, hidden), lambda i, r: (0, 0)),
            scratch_shapes=[pltpu.VMEM((1, hidden), jnp.float32), pltpu.SemaphoreType.DMA],
        ),
        out_shape=jax.ShapeDtypeStruct((own_nodes, hidden), jnp.bfloat16),
        compiler_params=pltpu.CompilerParams(vmem_limit_bytes=8 * 1024 * 1024),
    )(row, *operands, bias.reshape(1, hidden))


def solution(mesh):
    rows, cols = mesh.shape["row"], mesh.shape["col"]
    in_specs = (P("col", "row"), P(), P(), P("row", "col"), P("row", "col"), P("row", "col"))
    out_specs = P(("row", "col"), None)
    return jax.shard_map(
        functools.partial(body, rows, cols),
        mesh=mesh,
        in_specs=in_specs,
        out_specs=out_specs,
        check_vma=False,
    )
```

```python
import functools

import jax
import jax.numpy as jnp
from jax import lax
from jax.experimental import pallas as pl
from jax.experimental.pallas import tpu as pltpu
from jax.sharding import PartitionSpec as P

TILE = 128
LANES = 128
LOW = 256
NT = (((1,), (1,)), ((), ()))
BITS8 = jnp.float8_e4m3fn


def flag(condition):
    return jnp.where(condition, 1.0, 0.0).astype(jnp.bfloat16)


def short(whole):
    return whole.astype(jnp.float32).astype(jnp.bfloat16)


def equal(ids, whole):
    return jnp.where(ids == short(whole), jnp.bfloat16(1), jnp.bfloat16(0))


def pack_kernel(src_ref, dst_ref, count_ref, out_ref, lines):
    tiles, cap = src_ref.shape
    rows, cols, depth, _ = out_ref.shape
    subs = cap // LANES
    own = tiles // cols * subs // 2
    high = 2 * (depth - own)
    src = src_ref[...]
    tile_ids = lax.broadcasted_iota(jnp.int32, (tiles, cap), 0)
    count = jnp.zeros((tiles, cap), jnp.int32)
    for t in range(tiles):
        count = jnp.where(tile_ids == t, count_ref[t], count)
    live = lax.broadcasted_iota(jnp.int32, (tiles, cap), 1) < count
    packed = src + jnp.where(live, dst_ref[...], TILE) * 65536
    for j in range(subs):
        lines[pl.ds(j, tiles, stride=subs), :] = packed[:, j * LANES : (j + 1) * LANES]
    edges = lines[...].reshape(cols, 2 * own, LANES)
    for r in range(rows):
        first = r % 2 * own
        out_ref[r, :, :own, :] = edges[:, first : first + own, :]
    src_high = jnp.where(live, src // LANES, high)
    src_low = src % LANES
    high_ids = short(lax.broadcasted_iota(jnp.int32, (high, cap), 0))
    low_ids = short(lax.broadcasted_iota(jnp.int32, (LANES, cap), 0))
    total = jnp.zeros((high, LANES), jnp.float32)
    for t in range(tiles):
        total += lax.dot_general(
            equal(high_ids, src_high[t : t + 1]).astype(BITS8),
            equal(low_ids, src_low[t : t + 1]).astype(BITS8),
            NT,
            preferred_element_type=jnp.float32,
        )
    degree = total.astype(jnp.int32)
    for r in range(rows):
        first = r % 2 * (high // 2)
        out_ref[r, :, own:, :] = jnp.broadcast_to(
            degree[first : first + high // 2], (cols, high // 2, LANES)
        )


def ring_col_of(place, cols):
    return 2 * place if place < cols // 2 else 2 * (cols - 1 - place) + 1


def ring_place(col, cols):
    return jnp.where(col % 2 == 0, col // 2, cols - 1 - col // 2)


def ring_col(place, cols):
    return jnp.where(place < cols // 2, 2 * place, 2 * (cols - 1 - place) + 1)


def sum_kernel(cols, shifts, groups, first, last, col_ref, *refs):
    row_ref, *refs = refs
    edge_refs, refs = refs[:2], refs[2:]
    xs, refs = refs[: sum(groups)], refs[sum(groups) :]
    if not first:
        old_ref, old_degree_ref, *refs = refs
    rows, _, depth, _ = edge_refs[0].shape
    out_refs, (counts, scaled, total) = refs[:-3], refs[-3:]
    width = xs[0].shape[1]
    _, sums, src_rows = counts.shape
    highs = src_rows // LOW
    own = depth - src_rows // LANES // 2
    tiles = sums // rows // TILE // 2
    subs = own // tiles
    odd = lax.rem(row_ref[0], 2)
    place = ring_place(col_ref[0], cols)
    sign = 1 - 2 * lax.rem(place, 2)
    blocks = [ring_col(lax.rem(place + sign * shift + cols, cols), cols) for shift in shifts]
    diagonal = lax.broadcasted_iota(jnp.int32, (LANES, LANES), 0) == lax.broadcasted_iota(
        jnp.int32, (LANES, LANES), 1
    )
    target_ids = short(lax.broadcasted_iota(jnp.int32, (TILE, LANES), 0))
    low_ids = short(lax.broadcasted_iota(jnp.int32, (LOW, LANES), 0))

    def as_column(row):
        return jnp.sum(jnp.where(diagonal, row, 0.0), axis=1, keepdims=True)

    def put_scaled(g):
        halves = [
            sum(edge_ref[r, blocks[g], own:, :] for r in range(rows)).astype(jnp.float32)
            for edge_ref in edge_refs
        ]
        degree = jnp.where(odd == 0, jnp.concatenate(halves), jnp.concatenate(halves[::-1]))
        scale = lax.rsqrt(1.0 + degree)
        top = 0
        for x_ref in xs[sum(groups[:g]) : sum(groups[: g + 1])]:
            for i in range(x_ref.shape[0] // LANES):
                column = as_column(scale[top // LANES : top // LANES + 1])
                x = x_ref[i * LANES : (i + 1) * LANES, :].astype(jnp.float32)
                scaled[g % 2, top : top + LANES, :width] = (x * column).astype(jnp.bfloat16)
                top += LANES

    def count_block(g, edge_ref, r, t):
        lefts, rights = [], []
        for j in range(subs):
            edges = edge_ref[r, blocks[g], pl.ds(t * subs + j, 1), :]
            src = edges & 65535
            target_one = equal(target_ids, edges >> 16)
            src_high = src // LOW
            left = [target_one * flag(src_high == h) for h in range(highs)]
            lefts.append(jnp.concatenate(left, axis=0).astype(BITS8))
            rights.append(equal(low_ids, src % LOW).astype(BITS8))
        return lax.dot_general(
            jnp.concatenate(lefts, axis=1),
            jnp.concatenate(rights, axis=1),
            NT,
            preferred_element_type=jnp.float32,
        )

    def fill_part(g, part, convert, unroll):
        def fill_tile(i, carry):
            block = count_block(g, edge_refs[part], i // tiles, i % tiles)
            top = (part * rows * tiles + i) * TILE
            top = top if unroll else pl.multiple_of(top, TILE)
            for h in range(highs):
                counts[g % 2, pl.ds(top, TILE), h * LOW : (h + 1) * LOW] = convert(
                    block[h * TILE : (h + 1) * TILE]
                )
            return carry

        if unroll:
            for i in range(rows * tiles):
                fill_tile(i, 0)
        else:
            lax.fori_loop(0, rows * tiles, fill_tile, 0)

    def add_part(g, part, start):
        at = slice(part * (sums // 2), (part + 1) * (sums // 2))
        added = jnp.dot(counts[g % 2, at, :], scaled[g % 2], preferred_element_type=jnp.float32)
        total[at, :] = added if start else total[at, :] + added

    def rounded(block):
        return block.astype(jnp.bfloat16)

    def remainder(block):
        return (block - block.astype(jnp.bfloat16).astype(jnp.float32)).astype(jnp.bfloat16)

    scaled[...] = jnp.ones_like(scaled)
    unroll = rows * tiles <= 4
    for part in range(2):
        fill_part(0, part, rounded, unroll)
    put_scaled(0)
    for g in range(len(groups)):
        more = g + 1 < len(groups)
        for part in range(2):
            if more:
                fill_part(g + 1, part, rounded, unroll)
            add_part(g, part, g == 0)
        if more:
            put_scaled(g + 1)

    @pl.when(jnp.max(total[:, LANES:]) >= 256.0)
    def _():
        for g in range(len(groups)):
            put_scaled(g)
            for part in range(2):
                fill_part(g, part, remainder, False)
                add_part(g, part, False)

    if last:
        for shift in range(rows):
            r = row_ref[0] ^ shift
            for part in range(2):
                for t in range(tiles):
                    i = (part * rows + r) * tiles + t
                    at = pl.ds(pl.multiple_of(i * TILE, TILE), TILE)
                    value, degree = total[at, :width], total[at, LANES:]
                    if not first:
                        value += old_ref[at, :]
                        degree += as_column(old_degree_ref[pl.ds(i, 1), :])
                    half = 1 - odd if part else odd
                    place = pl.multiple_of((half * tiles + t) * TILE, TILE)
                    norm = lax.rsqrt(1.0 + degree[:, :width])
                    out_refs[shift][pl.ds(place, TILE), :] = (value * norm).astype(jnp.bfloat16)
    else:
        for i in range(sums // TILE):
            at = slice(i * TILE, (i + 1) * TILE)
            line = jnp.sum(jnp.where(diagonal, total[at, LANES:], 0.0), axis=0, keepdims=True)
            value = total[at, :width]
            out_refs[0][at, :] = value if first else value + old_ref[at, :]
            out_refs[1][i : i + 1, :] = line if first else line + old_degree_ref[i : i + 1, :]


def layer_kernel(row_ref, *refs):
    *x_refs, weight_ref, bias_hbm, out_ref, bias, arrived = refs
    copy = pltpu.make_async_copy(bias_hbm, bias, arrived)
    copy.start()
    rows, width = len(x_refs), x_refs[0].shape[1]
    projected = None
    for shift, x_ref in enumerate(x_refs):
        top = pl.multiple_of((row_ref[0] ^ shift) * width, width)
        part = jnp.dot(x_ref[...], weight_ref[pl.ds(top, width), :], preferred_element_type=jnp.float32)
        projected = part if projected is None else projected + part
    copy.wait()
    out_ref[...] = jnp.maximum(projected + bias[...], 0.0).astype(jnp.bfloat16)


def body(rows, cols, features, weight, bias, edge_src, edge_dst, tile_count):
    tiles, cap = edge_src.shape
    src_rows, width = features.shape
    hidden = weight.shape[1]
    degree_rows = src_rows // LANES
    own_rows = tiles * cap // LANES // cols
    own_nodes = tiles // cols * TILE
    sums = rows * own_nodes
    order = [ring_col_of(place, cols) for place in range(cols)]
    near = [(order[p], order[p ^ 1]) for p in range(cols)]
    next_near = [(order[p], order[((p + 1) % cols ^ 1) - 1]) for p in range(cols)]
    half = src_rows // 2

    depth = (own_rows + degree_rows) // 2
    packed = pl.pallas_call(
        pack_kernel,
        in_specs=[pl.BlockSpec(), pl.BlockSpec(), pl.BlockSpec(memory_space=pltpu.SMEM)],
        out_shape=jax.ShapeDtypeStruct((rows, cols, depth, LANES), jnp.int32),
        scratch_shapes=[pltpu.VMEM((cols * own_rows, LANES), jnp.int32)],
    )(edge_src, edge_dst, tile_count.reshape(tiles))
    edges = lax.all_to_all(
        packed.reshape(rows * cols, depth, LANES),
        ("row", "col"),
        split_axis=0,
        concat_axis=0,
        tiled=True,
    )
    other = lax.ppermute(edges, "row", [(r, r ^ 1) for r in range(rows)])
    edges = [half.reshape(rows, cols, depth, LANES) for half in (edges, other)]
    col = lax.axis_index("col").astype(jnp.int32).reshape(1)
    row = lax.axis_index("row").astype(jnp.int32).reshape(1)

    smem, vmem = pl.BlockSpec(memory_space=pltpu.SMEM), pl.BlockSpec(memory_space=pltpu.VMEM)

    def add_blocks(total, blocks, last, flops):
        first = total is None
        shifts = [shift for shift, _ in blocks]
        groups = [len(pieces) for _, pieces in blocks]
        pieces = [piece for _, listed in blocks for piece in listed]

        operands = pieces + ([] if first else list(total))
        out_shape = (
            [jax.ShapeDtypeStruct((own_nodes, width), jnp.bfloat16)] * rows
            if last
            else [
                jax.ShapeDtypeStruct((sums, width), jnp.float32),
                jax.ShapeDtypeStruct((sums // TILE, LANES), jnp.float32),
            ]
        )
        scratch = [
            pltpu.VMEM((2, sums, src_rows), jnp.bfloat16),
            pltpu.VMEM((2, src_rows, 2 * LANES), jnp.bfloat16),
            pltpu.VMEM((sums, 2 * LANES), jnp.float32),
        ]
        return pl.pallas_call(
            functools.partial(sum_kernel, cols, shifts, groups, first, last),
            in_specs=[smem] * 2 + [vmem] * (2 + len(operands)),
            out_specs=[vmem] * len(out_shape),
            scratch_shapes=scratch,
            out_shape=out_shape,
            compiler_params=pltpu.CompilerParams(vmem_limit_bytes=48 * 1024 * 1024),
            cost_estimate=pl.CostEstimate(flops=flops, bytes_accessed=2**22, transcendentals=0),
        )(col, row, *edges, *operands)

    block_flops = 2 * sums * src_rows * (2 * LANES + cap)
    here = there = features
    total, waiting = None, [(0, [features])]
    for hop in range(1, cols // 2):
        here, there = lax.ppermute(there, "col", near), lax.ppermute(here, "col", next_near)
        waiting += [(hop, [here]), (-hop, [there])]
        if hop > 1:
            total = add_blocks(total, waiting, False, 2 * len(waiting) * block_flops)
            waiting = []
    upper = lax.ppermute(there[:half], "col", near)
    lower = lax.ppermute(here[half:], "col", next_near)
    waiting.append((cols // 2, [upper, lower]))
    normed = add_blocks(total, waiting, True, block_flops)
    normed = [normed[0]] + [
        lax.ppermute(normed[shift], "row", [(r, r ^ shift) for r in range(rows)])
        for shift in range(1, rows)
    ]
    operands = [*normed, weight]
    return pl.pallas_call(
        layer_kernel,
        grid_spec=pltpu.PrefetchScalarGridSpec(
            num_scalar_prefetch=1,
            grid=(1,),
            in_specs=[pl.BlockSpec(array.shape, lambda i, r: (0, 0)) for array in operands]
            + [pl.BlockSpec(memory_space=pl.ANY)],
            out_specs=pl.BlockSpec((own_nodes, hidden), lambda i, r: (0, 0)),
            scratch_shapes=[pltpu.VMEM((1, hidden), jnp.float32), pltpu.SemaphoreType.DMA],
        ),
        out_shape=jax.ShapeDtypeStruct((own_nodes, hidden), jnp.bfloat16),
        compiler_params=pltpu.CompilerParams(vmem_limit_bytes=8 * 1024 * 1024),
    )(row, *operands, bias.reshape(1, hidden))


def solution(mesh):
    rows, cols = mesh.shape["row"], mesh.shape["col"]
    in_specs = (P("col", "row"), P(), P(), P("row", "col"), P("row", "col"), P("row", "col"))
    out_specs = P(("row", "col"), None)
    return jax.shard_map(
        functools.partial(body, rows, cols),
        mesh=mesh,
        in_specs=in_specs,
        out_specs=out_specs,
        check_vma=False,
    )
```

```python
import functools

import jax
import jax.numpy as jnp
from jax import lax
from jax.experimental import pallas as pl
from jax.experimental.pallas import tpu as pltpu
from jax.sharding import PartitionSpec as P

TILE = 128
LANES = 128
LOW = 256
NT = (((1,), (1,)), ((), ()))
BITS8 = jnp.float8_e4m3fn


def flag(condition):
    return jnp.where(condition, 1.0, 0.0).astype(jnp.bfloat16)


def short(whole):
    return whole.astype(jnp.float32).astype(jnp.bfloat16)


def equal(ids, whole):
    return jnp.where(ids == short(whole), jnp.bfloat16(1), jnp.bfloat16(0))


def pack_kernel(src_ref, dst_ref, count_ref, out_ref, lines):
    tiles, cap = src_ref.shape
    rows, cols, depth, _ = out_ref.shape
    subs = cap // LANES
    own = tiles // cols * subs // 2
    high = 2 * (depth - own)
    src = src_ref[...]
    tile_ids = lax.broadcasted_iota(jnp.int32, (tiles, cap), 0)
    count = jnp.zeros((tiles, cap), jnp.int32)
    for t in range(tiles):
        count = jnp.where(tile_ids == t, count_ref[t], count)
    live = lax.broadcasted_iota(jnp.int32, (tiles, cap), 1) < count
    packed = src + jnp.where(live, dst_ref[...], TILE) * 65536
    for j in range(subs):
        lines[pl.ds(j, tiles, stride=subs), :] = packed[:, j * LANES : (j + 1) * LANES]
    edges = lines[...].reshape(cols, 2 * own, LANES)
    for r in range(rows):
        first = r % 2 * own
        out_ref[r, :, :own, :] = edges[:, first : first + own, :]
    src_high = jnp.where(live, src // LANES, high)
    src_low = src % LANES
    high_ids = short(lax.broadcasted_iota(jnp.int32, (high, cap), 0))
    low_ids = short(lax.broadcasted_iota(jnp.int32, (LANES, cap), 0))
    total = jnp.zeros((high, LANES), jnp.float32)
    for t in range(tiles):
        total += lax.dot_general(
            equal(high_ids, src_high[t : t + 1]).astype(BITS8),
            equal(low_ids, src_low[t : t + 1]).astype(BITS8),
            NT,
            preferred_element_type=jnp.float32,
        )
    degree = total.astype(jnp.int32)
    for r in range(rows):
        first = r % 2 * (high // 2)
        out_ref[r, :, own:, :] = jnp.broadcast_to(
            degree[first : first + high // 2], (cols, high // 2, LANES)
        )


def ring_col_of(place, cols):
    return 2 * place if place < cols // 2 else 2 * (cols - 1 - place) + 1


def ring_place(col, cols):
    return jnp.where(col % 2 == 0, col // 2, cols - 1 - col // 2)


def ring_col(place, cols):
    return jnp.where(place < cols // 2, 2 * place, 2 * (cols - 1 - place) + 1)


def sum_kernel(cols, shifts, groups, first, last, col_ref, *refs):
    row_ref, *refs = refs
    edge_refs, refs = refs[:2], refs[2:]
    xs, refs = refs[: sum(groups)], refs[sum(groups) :]
    if not first:
        old_ref, old_degree_ref, *refs = refs
    rows, _, depth, _ = edge_refs[0].shape
    out_refs, (counts, scaled, total) = refs[:-3], refs[-3:]
    width = xs[0].shape[1]
    _, sums, src_rows = counts.shape
    highs = src_rows // LOW
    own = depth - src_rows // LANES // 2
    tiles = sums // rows // TILE // 2
    subs = own // tiles
    odd = lax.rem(row_ref[0], 2)
    place = ring_place(col_ref[0], cols)
    sign = 1 - 2 * lax.rem(place, 2)
    blocks = [ring_col(lax.rem(place + sign * shift + cols, cols), cols) for shift in shifts]
    diagonal = lax.broadcasted_iota(jnp.int32, (LANES, LANES), 0) == lax.broadcasted_iota(
        jnp.int32, (LANES, LANES), 1
    )
    target_ids = short(lax.broadcasted_iota(jnp.int32, (TILE, LANES), 0))
    low_ids = short(lax.broadcasted_iota(jnp.int32, (LOW, LANES), 0))

    def as_column(row):
        return jnp.sum(jnp.where(diagonal, row, 0.0), axis=1, keepdims=True)

    def put_scaled(g):
        halves = [
            sum(edge_ref[r, blocks[g], own:, :] for r in range(rows)).astype(jnp.float32)
            for edge_ref in edge_refs
        ]
        degree = jnp.where(odd == 0, jnp.concatenate(halves), jnp.concatenate(halves[::-1]))
        scale = lax.rsqrt(1.0 + degree)
        top = 0
        for x_ref in xs[sum(groups[:g]) : sum(groups[: g + 1])]:
            for i in range(x_ref.shape[0] // LANES):
                column = as_column(scale[top // LANES : top // LANES + 1])
                x = x_ref[i * LANES : (i + 1) * LANES, :].astype(jnp.float32)
                scaled[g % 2, top : top + LANES, :width] = (x * column).astype(jnp.bfloat16)
                top += LANES

    def count_block(g, edge_ref, r, t):
        lefts, rights = [], []
        for j in range(subs):
            edges = edge_ref[r, blocks[g], pl.ds(t * subs + j, 1), :]
            src = edges & 65535
            target_one = equal(target_ids, edges >> 16)
            src_high = src // LOW
            left = [target_one * flag(src_high == h) for h in range(highs)]
            lefts.append(jnp.concatenate(left, axis=0).astype(BITS8))
            rights.append(equal(low_ids, src % LOW).astype(BITS8))
        return lax.dot_general(
            jnp.concatenate(lefts, axis=1),
            jnp.concatenate(rights, axis=1),
            NT,
            preferred_element_type=jnp.float32,
        )

    def fill_part(g, part, convert, unroll):
        def fill_tile(i, carry):
            block = count_block(g, edge_refs[part], i // tiles, i % tiles)
            top = (part * rows * tiles + i) * TILE
            top = top if unroll else pl.multiple_of(top, TILE)
            for h in range(highs):
                counts[g % 2, pl.ds(top, TILE), h * LOW : (h + 1) * LOW] = convert(
                    block[h * TILE : (h + 1) * TILE]
                )
            return carry

        if unroll:
            for i in range(rows * tiles):
                fill_tile(i, 0)
        else:
            lax.fori_loop(0, rows * tiles, fill_tile, 0)

    def add_part(g, part, start):
        at = slice(part * (sums // 2), (part + 1) * (sums // 2))
        added = jnp.dot(counts[g % 2, at, :], scaled[g % 2], preferred_element_type=jnp.float32)
        total[at, :] = added if start else total[at, :] + added

    def rounded(block):
        return block.astype(jnp.bfloat16)

    def remainder(block):
        return (block - block.astype(jnp.bfloat16).astype(jnp.float32)).astype(jnp.bfloat16)

    scaled[...] = jnp.ones_like(scaled)
    unroll = rows * tiles <= 4
    for part in range(2):
        fill_part(0, part, rounded, unroll)
    put_scaled(0)
    for g in range(len(groups)):
        more = g + 1 < len(groups)
        for part in range(2):
            if more:
                fill_part(g + 1, part, rounded, unroll)
            if more and part:
                put_scaled(g + 1)
            add_part(g, part, g == 0)

    @pl.when(jnp.max(total[:, LANES:]) >= 256.0)
    def _():
        for g in range(len(groups)):
            put_scaled(g)
            for part in range(2):
                fill_part(g, part, remainder, False)
                add_part(g, part, False)

    if last:
        for shift in range(rows):
            r = row_ref[0] ^ shift
            for part in range(2):
                for t in range(tiles):
                    i = (part * rows + r) * tiles + t
                    at = pl.ds(pl.multiple_of(i * TILE, TILE), TILE)
                    value, degree = total[at, :width], total[at, LANES:]
                    if not first:
                        value += old_ref[at, :]
                        degree += as_column(old_degree_ref[pl.ds(i, 1), :])
                    half = 1 - odd if part else odd
                    place = pl.multiple_of((half * tiles + t) * TILE, TILE)
                    norm = lax.rsqrt(1.0 + degree[:, :width])
                    out_refs[shift][pl.ds(place, TILE), :] = (value * norm).astype(jnp.bfloat16)
    else:
        for i in range(sums // TILE):
            at = slice(i * TILE, (i + 1) * TILE)
            line = jnp.sum(jnp.where(diagonal, total[at, LANES:], 0.0), axis=0, keepdims=True)
            value = total[at, :width]
            out_refs[0][at, :] = value if first else value + old_ref[at, :]
            out_refs[1][i : i + 1, :] = line if first else line + old_degree_ref[i : i + 1, :]


def layer_kernel(row_ref, *refs):
    *x_refs, weight_ref, bias_hbm, out_ref, bias, arrived = refs
    copy = pltpu.make_async_copy(bias_hbm, bias, arrived)
    copy.start()
    rows, width = len(x_refs), x_refs[0].shape[1]
    projected = None
    for shift, x_ref in enumerate(x_refs):
        top = pl.multiple_of((row_ref[0] ^ shift) * width, width)
        part = jnp.dot(x_ref[...], weight_ref[pl.ds(top, width), :], preferred_element_type=jnp.float32)
        projected = part if projected is None else projected + part
    copy.wait()
    out_ref[...] = jnp.maximum(projected + bias[...], 0.0).astype(jnp.bfloat16)


def body(rows, cols, features, weight, bias, edge_src, edge_dst, tile_count):
    tiles, cap = edge_src.shape
    src_rows, width = features.shape
    hidden = weight.shape[1]
    degree_rows = src_rows // LANES
    own_rows = tiles * cap // LANES // cols
    own_nodes = tiles // cols * TILE
    sums = rows * own_nodes
    order = [ring_col_of(place, cols) for place in range(cols)]
    near = [(order[p], order[p ^ 1]) for p in range(cols)]
    next_near = [(order[p], order[((p + 1) % cols ^ 1) - 1]) for p in range(cols)]
    half = src_rows // 2

    depth = (own_rows + degree_rows) // 2
    packed = pl.pallas_call(
        pack_kernel,
        in_specs=[pl.BlockSpec(), pl.BlockSpec(), pl.BlockSpec(memory_space=pltpu.SMEM)],
        out_shape=jax.ShapeDtypeStruct((rows, cols, depth, LANES), jnp.int32),
        scratch_shapes=[pltpu.VMEM((cols * own_rows, LANES), jnp.int32)],
    )(edge_src, edge_dst, tile_count.reshape(tiles))
    edges = lax.all_to_all(
        packed.reshape(rows * cols, depth, LANES),
        ("row", "col"),
        split_axis=0,
        concat_axis=0,
        tiled=True,
    )
    other = lax.ppermute(edges, "row", [(r, r ^ 1) for r in range(rows)])
    edges = [half.reshape(rows, cols, depth, LANES) for half in (edges, other)]
    col = lax.axis_index("col").astype(jnp.int32).reshape(1)
    row = lax.axis_index("row").astype(jnp.int32).reshape(1)

    smem, vmem = pl.BlockSpec(memory_space=pltpu.SMEM), pl.BlockSpec(memory_space=pltpu.VMEM)

    def add_blocks(total, blocks, last, flops):
        first = total is None
        shifts = [shift for shift, _ in blocks]
        groups = [len(pieces) for _, pieces in blocks]
        pieces = [piece for _, listed in blocks for piece in listed]

        operands = pieces + ([] if first else list(total))
        out_shape = (
            [jax.ShapeDtypeStruct((own_nodes, width), jnp.bfloat16)] * rows
            if last
            else [
                jax.ShapeDtypeStruct((sums, width), jnp.float32),
                jax.ShapeDtypeStruct((sums // TILE, LANES), jnp.float32),
            ]
        )
        scratch = [
            pltpu.VMEM((2, sums, src_rows), jnp.bfloat16),
            pltpu.VMEM((2, src_rows, 2 * LANES), jnp.bfloat16),
            pltpu.VMEM((sums, 2 * LANES), jnp.float32),
        ]
        return pl.pallas_call(
            functools.partial(sum_kernel, cols, shifts, groups, first, last),
            in_specs=[smem] * 2 + [vmem] * (2 + len(operands)),
            out_specs=[vmem] * len(out_shape),
            scratch_shapes=scratch,
            out_shape=out_shape,
            compiler_params=pltpu.CompilerParams(vmem_limit_bytes=48 * 1024 * 1024),
            cost_estimate=pl.CostEstimate(flops=flops, bytes_accessed=2**22, transcendentals=0),
        )(col, row, *edges, *operands)

    block_flops = 2 * sums * src_rows * (2 * LANES + cap)
    here = there = features
    total, waiting = None, [(0, [features])]
    for hop in range(1, cols // 2):
        here, there = lax.ppermute(there, "col", near), lax.ppermute(here, "col", next_near)
        waiting += [(hop, [here]), (-hop, [there])]
        if hop > 1:
            total = add_blocks(total, waiting, False, 2 * len(waiting) * block_flops)
            waiting = []
    upper = lax.ppermute(there[:half], "col", near)
    lower = lax.ppermute(here[half:], "col", next_near)
    waiting.append((cols // 2, [upper, lower]))
    normed = add_blocks(total, waiting, True, block_flops)
    normed = [normed[0]] + [
        lax.ppermute(normed[shift], "row", [(r, r ^ shift) for r in range(rows)])
        for shift in range(1, rows)
    ]
    operands = [*normed, weight]
    return pl.pallas_call(
        layer_kernel,
        grid_spec=pltpu.PrefetchScalarGridSpec(
            num_scalar_prefetch=1,
            grid=(1,),
            in_specs=[pl.BlockSpec(array.shape, lambda i, r: (0, 0)) for array in operands]
            + [pl.BlockSpec(memory_space=pl.ANY)],
            out_specs=pl.BlockSpec((own_nodes, hidden), lambda i, r: (0, 0)),
            scratch_shapes=[pltpu.VMEM((1, hidden), jnp.float32), pltpu.SemaphoreType.DMA],
        ),
        out_shape=jax.ShapeDtypeStruct((own_nodes, hidden), jnp.bfloat16),
        compiler_params=pltpu.CompilerParams(vmem_limit_bytes=8 * 1024 * 1024),
    )(row, *operands, bias.reshape(1, hidden))


def solution(mesh):
    rows, cols = mesh.shape["row"], mesh.shape["col"]
    in_specs = (P("col", "row"), P(), P(), P("row", "col"), P("row", "col"), P("row", "col"))
    out_specs = P(("row", "col"), None)
    return jax.shard_map(
        functools.partial(body, rows, cols),
        mesh=mesh,
        in_specs=in_specs,
        out_specs=out_specs,
        check_vma=False,
    )
```
